256 devices in a mesh: blk: 32 (over z, x_hi, core), tp: 8 (over x_lo, y).
Axes of the slice: x: 4 (x_hi: 2, x_lo: 2; x = x_hi * 2 + x_lo), y: 4, z: 8, core: 2. Of those that a mesh axis runs over, the one named last changes fastest.
Arguments:
- queries: bfloat16 [16384, 8192], P('blk', 'tp'), may hold values from -6 to 6
- key_matrix: bfloat16 [16384, 1024], P('blk', 'tp'), may hold values from -6 to 6
- value_matrix: bfloat16 [16384, 1024], P('blk', 'tp'), may hold values from -6 to 6
- attention_output: bfloat16 [16384, 8192], P('blk', 'tp'), may hold values from -1.5 to 1.5
- output_gradient: bfloat16 [16384, 8192], P('blk', 'tp'), may hold values from -24 to 24
- softmax_log_total: float32 [64, 16384], P('tp', 'blk'), may hold values from 5 to 7.5
- positions: int32 [16384], P(('blk', 'tp')), may hold values from 0 to 16383, as said below
Outputs:
- query_grad: bfloat16 [16384, 8192], P('blk', 'tp')
- key_gradient: bfloat16 [16384, 1024], P('blk', 'tp')
- value_gradient: bfloat16 [16384, 1024], P('blk', 'tp')
The draws below stay inside these ranges and needn't reach their ends.
Inputs may be any that keep to these rules, and one draw needn't show every extreme that they name: Every position occurs once. Block b (tokens b * 512 to b * 512 + 511) holds two runs of 256 consecutive positions in rising order: first piece c, then piece 2 * 32 - 1 - c, where piece m is positions m * 256 to (m + 1) * 256 - 1, and the c of the blocks are distinct.
All inputs are finite; a program needn't handle non-finite values.
Results may differ from the reference program's by a relative error of at most 0.0051.
Values may be sent and summed in bfloat16 or wider, within the bound.
No kernel may reach another device: no remote copies, remote signals or barrier semaphores. Data moves between devices by JAX's collectives and lax.ppermute only.
A program may use at most 64 MiB of HBM per device.

```python
import math
import jax
import jax.numpy as jnp
from jax import lax

QUERY_HEADS = 64
KEY_VALUE_HEADS = 8
HEAD_SIZE = 128
BLOCK_TOKENS = 512
STEPS = 2
SEQUENCE_TOKENS = 16384
N_BLK = 32


def draw_positions(key, part):
    key = jax.random.fold_in(key, 11)
    piece_order = jax.random.permutation(key, N_BLK).astype(jnp.int32)
    half_len = BLOCK_TOKENS // 2
    token_index = jnp.arange(SEQUENCE_TOKENS, dtype=jnp.int32)
    block_index = token_index // BLOCK_TOKENS
    within_block = token_index % BLOCK_TOKENS
    low_piece = piece_order[block_index]
    piece_index = jnp.where(within_block < half_len, low_piece, 2 * N_BLK - 1 - low_piece)
    return (piece_index * half_len + within_block % half_len).astype(jnp.int32)


def steps_of(rng, dims, pieces, least, high):
    loudness = 1.0
    for position, parts in pieces:
        heights = jax.random.uniform(jax.random.fold_in(jax.random.fold_in(rng, 6), position), (parts,), jnp.float32, least / len(pieces), high / len(pieces))
        loudness = loudness * jnp.repeat(jnp.exp(heights), dims[position] // parts).reshape((-1,) + (1,) * (len(dims) - 1 - position))
    return loudness


def gaussian(key, shape, spread, bound, pieces=(), held_as=jnp.bfloat16):
    result = jax.random.normal(key, shape, jnp.float32) * spread
    if len(pieces) > 0:
        result = steps_of(key, shape, pieces, -0.22, 0.18) * result
    return jnp.clip(result, min=-bound, max=bound).astype(held_as)


def setup_inputs(seed: int = 0) -> dict:
    splits = jax.random.split(jax.random.key(seed), 8)
    return {
        "queries": gaussian(splits[0], (SEQUENCE_TOKENS, QUERY_HEADS * HEAD_SIZE), 1.0, 6.0, ((0, 32), (1, 8))),
        "key_matrix": gaussian(splits[1], (SEQUENCE_TOKENS, KEY_VALUE_HEADS * HEAD_SIZE), 1.0, 6.0, ((0, 32), (1, 8))),
        "value_matrix": gaussian(splits[2], (SEQUENCE_TOKENS, KEY_VALUE_HEADS * HEAD_SIZE), 1.0, 6.0, ((0, 32), (1, 8))),
        "attention_output": gaussian(splits[3], (SEQUENCE_TOKENS, QUERY_HEADS * HEAD_SIZE), 0.25, 1.5, ((0, 32), (1, 8))),
        "output_gradient": gaussian(splits[4], (SEQUENCE_TOKENS, QUERY_HEADS * HEAD_SIZE), 4.0, 24.0, ((0, 32), (1, 8))),
        "softmax_log_total": jnp.clip(5.0 + 2.5 * jax.random.uniform(splits[5], (QUERY_HEADS, SEQUENCE_TOKENS), jnp.float32) ** steps_of(splits[5], (QUERY_HEADS, SEQUENCE_TOKENS), ((0, 8), (1, 32)), -0.2, 0.2), 5.0, 7.5),
        "positions": draw_positions(jax.random.fold_in(splits[7], 71), 0),
    }


def reference(queries, key_matrix, value_matrix, attention_output, output_gradient, softmax_log_total, positions):
    block_count = SEQUENCE_TOKENS // BLOCK_TOKENS
    query_group_width = QUERY_HEADS // KEY_VALUE_HEADS
    score_scale = 1.0 / math.sqrt(HEAD_SIZE)
    query_split_view = queries.reshape(block_count, BLOCK_TOKENS, KEY_VALUE_HEADS, query_group_width, HEAD_SIZE)
    output_grad_split = output_gradient.reshape(block_count, BLOCK_TOKENS, KEY_VALUE_HEADS, query_group_width, HEAD_SIZE)
    output_split_view = attention_output.reshape(block_count, BLOCK_TOKENS, KEY_VALUE_HEADS, query_group_width, HEAD_SIZE)
    key_split_view = key_matrix.reshape(block_count, BLOCK_TOKENS, KEY_VALUE_HEADS, HEAD_SIZE)
    value_split_view = value_matrix.reshape(block_count, BLOCK_TOKENS, KEY_VALUE_HEADS, HEAD_SIZE)
    log_total_split = softmax_log_total.reshape(KEY_VALUE_HEADS, query_group_width, block_count, BLOCK_TOKENS)
    place_rows = positions.reshape(block_count, BLOCK_TOKENS)

    def one_block(carry, block):
        key_grad_running, value_grad_running = carry
        query_here = query_split_view[block].astype(jnp.float32)
        grad_here = output_grad_split[block].astype(jnp.float32)
        row_dot = lax.optimization_barrier(jnp.sum(grad_here * output_split_view[block].astype(jnp.float32), axis=3)).transpose(1, 2, 0)
        norm_here = lax.dynamic_index_in_dim(log_total_split, block, axis=2, keepdims=False)
        own_pos = place_rows[block]
        query_grad_running = jnp.zeros((BLOCK_TOKENS, KEY_VALUE_HEADS, query_group_width, HEAD_SIZE), jnp.float32)
        for offset in range(STEPS + 1):
            source = ((block - offset) % block_count).astype(jnp.int32)
            key_here = key_split_view[source].astype(jnp.float32)
            value_here = value_split_view[source].astype(jnp.float32)
            allowed = place_rows[source][None, :] <= own_pos[:, None]
            scores = jnp.einsum('ikgd,jkd->kgij', query_here, key_here) * score_scale
            weights = jnp.where(allowed, jnp.exp(scores - norm_here[..., None]), 0.0)
            rounded = lax.optimization_barrier(weights.astype(jnp.bfloat16)).astype(jnp.float32)
            value_part = jnp.einsum('kgij,ikgd->jkd', rounded, grad_here)
            grad_weights = jnp.einsum('ikgd,jkd->kgij', grad_here, value_here)
            grad_scores = (weights * (grad_weights - row_dot[..., None])).astype(jnp.bfloat16)
            grad_scores = lax.optimization_barrier(grad_scores).astype(jnp.float32)
            query_grad_running = query_grad_running + jnp.einsum('kgij,jkd->ikgd', grad_scores, key_here) * score_scale
            key_part = jnp.einsum('kgij,ikgd->jkd', grad_scores, query_here) * score_scale
            key_grad_running = key_grad_running.at[source].add(key_part)
            value_grad_running = value_grad_running.at[source].add(value_part)
        return ((key_grad_running, value_grad_running), query_grad_running.astype(jnp.bfloat16))
    block_begin = jnp.zeros((block_count, BLOCK_TOKENS, KEY_VALUE_HEADS, HEAD_SIZE), jnp.float32)
    (key_grad_running, value_grad_running), query_blocks = lax.scan(one_block, (block_begin, block_begin), jnp.arange(block_count, dtype=jnp.int32))
    query_grad = query_blocks.reshape(SEQUENCE_TOKENS, QUERY_HEADS * HEAD_SIZE)
    key_gradient = key_grad_running.reshape(SEQUENCE_TOKENS, KEY_VALUE_HEADS * HEAD_SIZE).astype(jnp.bfloat16)
    value_gradient = value_grad_running.reshape(SEQUENCE_TOKENS, KEY_VALUE_HEADS * HEAD_SIZE).astype(jnp.bfloat16)
    return (query_grad, key_gradient, value_gradient)
```

```python
import functools
import math

import jax
import jax.numpy as jnp
from jax import lax
from jax.experimental import pallas as pl
from jax.experimental.pallas import tpu as pltpu
from jax.sharding import PartitionSpec as P

D = 128
H = 8
T = 512
HALF = T // 2
PIECES = 64
GROUP = 4
SCALE = 1.0 / math.sqrt(D)
LOG2E = math.log2(math.e)
SCORE_SCALE = SCALE * LOG2E
F32 = jnp.float32
BF16 = jnp.bfloat16


def dot(a, b):
    return lax.dot_general(a, b, (((1,), (0,)), ((), ())), preferred_element_type=F32)


def dot_t(a, b):
    return lax.dot_general(a, b, (((1,), (1,)), ((), ())), preferred_element_type=F32)


def cat(parts, axis):
    return parts[0] if len(parts) == 1 else jnp.concatenate(parts, axis)


def add(total, part):
    return part if total is None else total + part


def weights_of(q, g, k_t, v_t, log_total, row_dot, mask):
    p = jnp.exp2(dot(q, k_t) * SCORE_SCALE - log_total)
    if mask is not None:
        p = jnp.where(mask, p, 0.0)
    ds = p * (dot(g, v_t) - row_dot)
    return p.astype(BF16), ds.astype(BF16)


def own_kernel(off, q_ref, g_ref, o_ref, l_ref, k_ref, v_ref, dq_ref, dkv_ref, stat_ref, stat_t):
    ql = pl.multiple_of(off[0], HALF)
    qh = pl.multiple_of(HALF - off[0], HALF)
    rows = lax.broadcasted_iota(jnp.int32, (H, 2 * D), 0)
    row_dot = jnp.zeros((H, T), F32)
    for h in range(H):
        cols = slice(h * D, (h + 1) * D)
        prod = g_ref[:, cols].astype(F32) * o_ref[:, cols].astype(F32)
        top = prod.astype(BF16)
        rest = (prod - top.astype(F32)).astype(BF16)
        pick = jnp.where(rows == h, 1.0, 0.0).astype(BF16)
        row_dot += dot_t(pick, jnp.concatenate([top, rest], 1))
    stat = jnp.concatenate([l_ref[...] * LOG2E, row_dot], 0)
    stat_ref[...] = stat
    stat_t[...] = stat.T
    mask = lax.broadcasted_iota(jnp.int32, (HALF, HALF), 1) <= lax.broadcasted_iota(
        jnp.int32, (HALF, HALF), 0
    )
    kl, kh = k_ref[pl.ds(ql, HALF), :], k_ref[pl.ds(qh, HALF), :]
    vl, vh = v_ref[pl.ds(ql, HALF), :], v_ref[pl.ds(qh, HALF), :]
    kl_t, kh_t, vl_t, vh_t = kl.T, kh.T, vl.T, vh.T
    k_both = jnp.concatenate([kl, kh], 0)
    dk_l = dk_h = dv_l = dv_h = None
    for h0 in range(0, H, GROUP):
        p_l, p_h, d_l, d_h, g_l, g_h, q_l, q_h = [], [], [], [], [], [], [], []
        for h in range(h0, h0 + GROUP):
            cols = slice(h * D, (h + 1) * D)
            q0, q1 = q_ref[pl.ds(ql, HALF), cols], q_ref[pl.ds(qh, HALF), cols]
            g0, g1 = g_ref[pl.ds(ql, HALF), cols], g_ref[pl.ds(qh, HALF), cols]
            l0, l1 = stat_t[pl.ds(ql, HALF), h : h + 1], stat_t[pl.ds(qh, HALF), h : h + 1]
            r0 = stat_t[pl.ds(ql, HALF), H + h : H + h + 1]
            r1 = stat_t[pl.ds(qh, HALF), H + h : H + h + 1]
            p00, d00 = weights_of(q0, g0, kl_t, vl_t, l0, r0, mask)
            p10, d10 = weights_of(q1, g1, kl_t, vl_t, l1, r1, None)
            p11, d11 = weights_of(q1, g1, kh_t, vh_t, l1, r1, mask)
            q0_t, q1_t, g0_t, g1_t = q0.T, q1.T, g0.T, g1.T
            p_l += [p00, p10]
            d_l += [d00, d10]
            p_h += [p11]
            d_h += [d11]
            g_l += [g0_t, g1_t]
            q_l += [q0_t, q1_t]
            g_h += [g1_t]
            q_h += [q1_t]
            dq_ref[pl.ds(ql, HALF), cols] = dot(d00, kl)
            dq_ref[pl.ds(qh, HALF), cols] = dot(jnp.concatenate([d10, d11], 1), k_both)
        dv_l = add(dv_l, dot(cat(g_l, 1), cat(p_l, 0)))
        dv_h = add(dv_h, dot(cat(g_h, 1), cat(p_h, 0)))
        dk_l = add(dk_l, dot(cat(q_l, 1), cat(d_l, 0)))
        dk_h = add(dk_h, dot(cat(q_h, 1), cat(d_h, 0)))
    dkv_ref[pl.ds(ql, HALF), :] = (dk_l * SCALE).T
    dkv_ref[pl.ds(qh, HALF), :] = (dk_h * SCALE).T
    dkv_ref[pl.ds(pl.multiple_of(T + ql, HALF), HALF), :] = dv_l.T
    dkv_ref[pl.ds(pl.multiple_of(T + qh, HALF), HALF), :] = dv_h.T


def other_kernel(last, ids, q_ref, g_ref, stat_ref, k_ref, v_ref, part_ref, dq_ref, dkv_ref, stat_t):
    ql = pl.multiple_of(ids[0], HALF)
    qh = pl.multiple_of(HALF - ids[0], HALF)
    kl = pl.multiple_of(ids[1], HALF)
    kh = pl.multiple_of(HALF - ids[1], HALF)
    lows = ids[2]
    q2 = pl.multiple_of(jnp.where(lows == 1, ql, qh), HALF)
    k2 = pl.multiple_of(jnp.where(lows == 1, kl, kh), HALF)
    in_low = lows.astype(F32)
    in_high = 1.0 - in_low
    stat_t[...] = stat_ref[...].T
    ka, kb = k_ref[pl.ds(kl, HALF), :], k_ref[pl.ds(k2, HALF), :]
    va, vb = v_ref[pl.ds(kl, HALF), :], v_ref[pl.ds(k2, HALF), :]
    ka_t, kb_t, va_t, vb_t = ka.T, kb.T, va.T, vb.T
    dk_a = dk_b = dv_a = dv_b = None
    for h0 in range(0, H, GROUP):
        p_a, p_b, d_a, d_b, g_a, g_b, q_a, q_b = [], [], [], [], [], [], [], []
        for h in range(h0, h0 + GROUP):
            cols = slice(h * D, (h + 1) * D)

            def quadrant(rows, k_t, v_t, h=h, cols=cols):
                q, g = q_ref[pl.ds(rows, HALF), cols], g_ref[pl.ds(rows, HALF), cols]
                log_total = stat_t[pl.ds(rows, HALF), h : h + 1]
                row_dot = stat_t[pl.ds(rows, HALF), H + h : H + h + 1]
                p, ds = weights_of(q, g, k_t, v_t, log_total, row_dot, None)
                return p, ds, q.T, g.T

            p, da, q, g = quadrant(qh, ka_t, va_t)
            p_a, d_a, q_a, g_a = p_a + [p], d_a + [da], q_a + [q], g_a + [g]
            p, db, q, g = quadrant(q2, kb_t, vb_t)
            p_b, d_b, q_b, g_b = p_b + [p], d_b + [db], q_b + [q], g_b + [g]
            x1, x2 = dot(da, ka), dot(db, kb)
            high = part_ref[pl.ds(qh, HALF), cols] + (x1 + in_high * x2)
            low = part_ref[pl.ds(ql, HALF), cols] + in_low * x2
            if last:
                high, low = (high * SCALE).astype(BF16), (low * SCALE).astype(BF16)
            dq_ref[pl.ds(qh, HALF), cols] = high
            dq_ref[pl.ds(ql, HALF), cols] = low
        dv_a = add(dv_a, dot(cat(g_a, 1), cat(p_a, 0)))
        dv_b = add(dv_b, dot(cat(g_b, 1), cat(p_b, 0)))
        dk_a = add(dk_a, dot(cat(q_a, 1), cat(d_a, 0)))
        dk_b = add(dk_b, dot(cat(q_b, 1), cat(d_b, 0)))
    dk_a, dk_b = dk_a * SCALE, dk_b * SCALE
    dkv_ref[pl.ds(kl, HALF), :] = (dk_a + in_low * dk_b).T.astype(BF16)
    dkv_ref[pl.ds(kh, HALF), :] = (in_high * dk_b).T.astype(BF16)
    dkv_ref[pl.ds(pl.multiple_of(T + kl, HALF), HALF), :] = (dv_a + in_low * dv_b).T.astype(BF16)
    dkv_ref[pl.ds(pl.multiple_of(T + kh, HALF), HALF), :] = (in_high * dv_b).T.astype(BF16)


def vmem():
    return pl.BlockSpec(memory_space=pltpu.VMEM)


def smem():
    return pl.BlockSpec(memory_space=pltpu.SMEM)


def cost(quadrants, size):
    return pl.CostEstimate(
        flops=quadrants * H * 20 * HALF * HALF * D,
        bytes_accessed=size,
        transcendentals=quadrants * H * HALF * HALF,
    )


def own_block(off, q, g, o, l, k, v):
    return pl.pallas_call(
        own_kernel,
        in_specs=[smem()] + [vmem()] * 6,
        out_specs=[vmem()] * 3,
        out_shape=[
            jax.ShapeDtypeStruct((T, H * D), F32),
            jax.ShapeDtypeStruct((2 * T, D), F32),
            jax.ShapeDtypeStruct((2 * H, T), F32),
        ],
        scratch_shapes=[pltpu.VMEM((T, 2 * H), F32)],
        compiler_params=pltpu.CompilerParams(vmem_limit_bytes=24 << 20),
        cost_estimate=cost(3, 6 << 20),
        name="own_block",
    )(off, q, g, o, l, k, v)


def other_block(last, ids, q, g, stat, k, v, part):
    return pl.pallas_call(
        functools.partial(other_kernel, last),
        in_specs=[smem()] + [vmem()] * 6,
        out_specs=[vmem()] * 2,
        out_shape=[
            jax.ShapeDtypeStruct((T, H * D), BF16 if last else F32),
            jax.ShapeDtypeStruct((2 * T, D), BF16),
        ],
        scratch_shapes=[pltpu.VMEM((T, 2 * H), F32)],
        compiler_params=pltpu.CompilerParams(vmem_limit_bytes=24 << 20),
        cost_estimate=cost(2, 6 << 20),
        name="other_block",
    )(ids, q, g, stat, k, v, part)


def passed_along(value, steps):
    count = lax.axis_size("blk")
    pairs = [(source, (source + steps) % count) for source in range(count)]
    return lax.ppermute(value, "blk", pairs)


def swapped(value):
    count = lax.axis_size("blk")
    return lax.ppermute(value, "blk", [(source, source ^ 1) for source in range(count)])


def first_piece(positions):
    piece = positions[0] // HALF
    in_first = lax.axis_index("tp") < lax.axis_size("tp") // 2
    return jnp.where(in_first, piece, PIECES - 1 - piece)


def low_row(first):
    return jnp.where(first < PIECES // 2, 0, HALF).astype(jnp.int32)


def low_piece(first):
    return jnp.minimum(first, PIECES - 1 - first)


def on_device(q, k, v, o, g, log_total, positions):
    k_two, v_two, pos_two = passed_along(k, 2), passed_along(v, 2), passed_along(positions, 2)
    first = first_piece(positions)
    off = low_row(first)
    dq, dkv, stat = own_block(off.reshape(1), q, g, o, log_total, k, v)
    even = lax.axis_index("blk") % 2 == 0
    k_one, v_one, pos_one = (
        swapped(jnp.where(even, a, b))
        for a, b in ((k, k_two), (v, v_two), (positions, pos_two))
    )

    def ids(pos):
        theirs = first_piece(pos)
        lows = (low_piece(first) > low_piece(theirs)).astype(jnp.int32)
        return jnp.stack([off, low_row(theirs), lows])

    dq, dkv_two = other_block(False, ids(pos_two), q, g, stat, k_two, v_two, dq)
    back_two = passed_along(dkv_two, -2)
    dq, dkv_one = other_block(True, ids(pos_one), q, g, stat, k_one, v_one, dq)
    back_one = passed_along(dkv_one, -1)
    total = (dkv + back_two.astype(F32) + back_one.astype(F32)).astype(BF16)
    return dq, total[:T], total[T:]


def solution(mesh):
    in_specs = (
        P("blk", "tp"),
        P("blk", "tp"),
        P("blk", "tp"),
        P("blk", "tp"),
        P("blk", "tp"),
        P("tp", "blk"),
        P(("blk", "tp")),
    )
    out_specs = (P("blk", "tp"), P("blk", "tp"), P("blk", "tp"))
    return jax.shard_map(
        on_device, mesh=mesh, in_specs=in_specs, out_specs=out_specs, check_vma=False
    )
```

```python
import functools
import math

import jax
import jax.numpy as jnp
from jax import lax
from jax.experimental import pallas as pl
from jax.experimental.pallas import tpu as pltpu
from jax.sharding import PartitionSpec as P

D = 128
H = 8
T = 512
HALF = T // 2
PIECES = 64
IDS = 16
GROUP = 4
SCALE = 1.0 / math.sqrt(D)
LOG2E = math.log2(math.e)
SCORE_SCALE = SCALE * LOG2E
F32 = jnp.float32
BF16 = jnp.bfloat16


def dot(a, b):
    return lax.dot_general(a, b, (((1,), (0,)), ((), ())), preferred_element_type=F32)


def dot_t(a, b):
    return lax.dot_general(a, b, (((1,), (1,)), ((), ())), preferred_element_type=F32)


def cat(parts, axis):
    return parts[0] if len(parts) == 1 else jnp.concatenate(parts, axis)


def add(total, part):
    return part if total is None else total + part


def weights_of(q, g, k_t, v_t, log_total, row_dot, mask):
    p = jnp.exp2(dot(q, k_t) * SCORE_SCALE - log_total)
    if mask is not None:
        p = jnp.where(mask, p, 0.0)
    ds = p * (dot(g, v_t) - row_dot)
    return p.astype(BF16), ds.astype(BF16)


def piece_of(message):
    return jnp.max(message[2 * T :, :].astype(F32)).astype(jnp.int32)


def low_row(first):
    return pl.multiple_of(jnp.where(first < PIECES // 2, 0, HALF), HALF)


def low_piece(first):
    return jnp.minimum(first, PIECES - 1 - first)


def pack_kernel(k_hbm, v_hbm, pos_hbm, message, pos, sems):
    copies = [
        pltpu.make_async_copy(pos_hbm, pos, sems.at[0]),
        pltpu.make_async_copy(k_hbm, message.at[pl.ds(0, T), :], sems.at[1]),
        pltpu.make_async_copy(v_hbm, message.at[pl.ds(T, T), :], sems.at[2]),
    ]
    for copy in copies:
        copy.start()
    copies[0].wait()
    piece = pos[0] // HALF
    in_first = lax.axis_index("tp") < lax.axis_size("tp") // 2
    first = jnp.where(in_first, piece, PIECES - 1 - piece)
    message[2 * T :, :] = jnp.full((IDS, D), first.astype(F32), F32).astype(BF16)
    copies[1].wait()
    copies[2].wait()


def own_kernel(q_hbm, g_hbm, o_hbm, l_hbm, message, dq_ref, dkv_ref, stat_ref, q_ref, g_ref, o_ref, l_ref, stat_t, sems):
    loads = []
    for n, h0 in enumerate(range(0, H, GROUP)):
        cols = pl.ds(h0 * D, GROUP * D)
        loads.append(
            [
                pltpu.make_async_copy(source.at[:, cols], target.at[:, cols], sems.at[n, i])
                for i, (source, target) in enumerate(
                    ((g_hbm, g_ref), (o_hbm, o_ref), (q_hbm, q_ref))
                )
            ]
        )
    load_l = pltpu.make_async_copy(l_hbm, l_ref, sems.at[0, 3])
    load_l.start()
    for load in loads:
        for copy in load:
            copy.start()
    k_ref, v_ref = message.at[pl.ds(0, T), :], message.at[pl.ds(T, T), :]
    ql = low_row(piece_of(message))
    qh = pl.multiple_of(HALF - ql, HALF)
    rows = lax.broadcasted_iota(jnp.int32, (H, 2 * D), 0)
    mask = lax.broadcasted_iota(jnp.int32, (HALF, HALF), 1) <= lax.broadcasted_iota(
        jnp.int32, (HALF, HALF), 0
    )
    kl, kh = k_ref[pl.ds(ql, HALF), :], k_ref[pl.ds(qh, HALF), :]
    vl, vh = v_ref[pl.ds(ql, HALF), :], v_ref[pl.ds(qh, HALF), :]
    kl_t, kh_t, vl_t, vh_t = kl.T, kh.T, vl.T, vh.T
    k_both = jnp.concatenate([kl, kh], 0)
    dk_l = dk_h = dv_l = dv_h = None
    load_l.wait()
    for n, h0 in enumerate(range(0, H, GROUP)):
        for copy in loads[n]:
            copy.wait()
        row_dot = jnp.zeros((2 * GROUP, T), F32)
        for h in range(h0, h0 + GROUP):
            cols = slice(h * D, (h + 1) * D)
            prod = g_ref[:, cols].astype(F32) * o_ref[:, cols].astype(F32)
            top = prod.astype(BF16)
            rest = (prod - top.astype(F32)).astype(BF16)
            pick = jnp.where(rows == GROUP + h - h0, 1.0, 0.0).astype(BF16)
            row_dot += dot_t(pick, jnp.concatenate([top, rest], 1))
        stat = jnp.concatenate([l_ref[h0 : h0 + GROUP, :] * LOG2E, row_dot[GROUP:, :]], 0)
        stat_ref[2 * h0 : 2 * (h0 + GROUP), :] = stat
        stat_t[:, 2 * h0 : 2 * (h0 + GROUP)] = stat.T
        p_l, p_h, d_l, d_h, g_l, g_h, q_l, q_h = [], [], [], [], [], [], [], []
        for h in range(h0, h0 + GROUP):
            cols = slice(h * D, (h + 1) * D)
            q0, q1 = q_ref[pl.ds(ql, HALF), cols], q_ref[pl.ds(qh, HALF), cols]
            g0, g1 = g_ref[pl.ds(ql, HALF), cols], g_ref[pl.ds(qh, HALF), cols]
            at, to = h0 + h, h0 + h + GROUP
            l0, l1 = stat_t[pl.ds(ql, HALF), at : at + 1], stat_t[pl.ds(qh, HALF), at : at + 1]
            r0, r1 = stat_t[pl.ds(ql, HALF), to : to + 1], stat_t[pl.ds(qh, HALF), to : to + 1]
            p00, d00 = weights_of(q0, g0, kl_t, vl_t, l0, r0, mask)
            p10, d10 = weights_of(q1, g1, kl_t, vl_t, l1, r1, None)
            p11, d11 = weights_of(q1, g1, kh_t, vh_t, l1, r1, mask)
            q0_t, q1_t, g0_t, g1_t = q0.T, q1.T, g0.T, g1.T
            p_l += [p00, p10]
            d_l += [d00, d10]
            p_h += [p11]
            d_h += [d11]
            g_l += [g0_t, g1_t]
            q_l += [q0_t, q1_t]
            g_h += [g1_t]
            q_h += [q1_t]
            dq_ref[pl.ds(ql, HALF), cols] = dot(d00, kl)
            dq_ref[pl.ds(qh, HALF), cols] = dot(jnp.concatenate([d10, d11], 1), k_both)
        dv_l = add(dv_l, dot(cat(g_l, 1), cat(p_l, 0)))
        dv_h = add(dv_h, dot(cat(g_h, 1), cat(p_h, 0)))
        dk_l = add(dk_l, dot(cat(q_l, 1), cat(d_l, 0)))
        dk_h = add(dk_h, dot(cat(q_h, 1), cat(d_h, 0)))
    dkv_ref[pl.ds(ql, HALF), :] = (dk_l * SCALE).T
    dkv_ref[pl.ds(qh, HALF), :] = (dk_h * SCALE).T
    dkv_ref[pl.ds(pl.multiple_of(T + ql, HALF), HALF), :] = dv_l.T
    dkv_ref[pl.ds(pl.multiple_of(T + qh, HALF), HALF), :] = dv_h.T


def other_kernel(last, q_ref, g_ref, stat_ref, message, theirs, part_ref, dq_ref, dkv_ref, stat_t):
    own_first, their_first = piece_of(message), piece_of(theirs)
    k_ref, v_ref = theirs.at[pl.ds(0, T), :], theirs.at[pl.ds(T, T), :]
    ql, kl = low_row(own_first), low_row(their_first)
    qh, kh = pl.multiple_of(HALF - ql, HALF), pl.multiple_of(HALF - kl, HALF)
    lows = (low_piece(own_first) > low_piece(their_first)).astype(jnp.int32)
    q2 = pl.multiple_of(jnp.where(lows == 1, ql, qh), HALF)
    k2 = pl.multiple_of(jnp.where(lows == 1, kl, kh), HALF)
    in_low = lows.astype(F32)
    in_high = 1.0 - in_low
    stat_t[...] = stat_ref[...].T
    ka, kb = k_ref[pl.ds(kl, HALF), :], k_ref[pl.ds(k2, HALF), :]
    va, vb = v_ref[pl.ds(kl, HALF), :], v_ref[pl.ds(k2, HALF), :]
    ka_t, kb_t, va_t, vb_t = ka.T, kb.T, va.T, vb.T
    dk_a = dk_b = dv_a = dv_b = None
    for h0 in range(0, H, GROUP):
        p_a, p_b, d_a, d_b, g_a, g_b, q_a, q_b = [], [], [], [], [], [], [], []
        for h in range(h0, h0 + GROUP):
            cols = slice(h * D, (h + 1) * D)

            def quadrant(rows, k_t, v_t, h=h, cols=cols):
                q, g = q_ref[pl.ds(rows, HALF), cols], g_ref[pl.ds(rows, HALF), cols]
                at, to = h0 + h, h0 + h + GROUP
                log_total = stat_t[pl.ds(rows, HALF), at : at + 1]
                row_dot = stat_t[pl.ds(rows, HALF), to : to + 1]
                p, ds = weights_of(q, g, k_t, v_t, log_total, row_dot, None)
                return p, ds, q.T, g.T

            p, da, q, g = quadrant(qh, ka_t, va_t)
            p_a, d_a, q_a, g_a = p_a + [p], d_a + [da], q_a + [q], g_a + [g]
            p, db, q, g = quadrant(q2, kb_t, vb_t)
            p_b, d_b, q_b, g_b = p_b + [p], d_b + [db], q_b + [q], g_b + [g]
            x1, x2 = dot(da, ka), dot(db, kb)
            high = part_ref[pl.ds(qh, HALF), cols] + (x1 + in_high * x2)
            low = part_ref[pl.ds(ql, HALF), cols] + in_low * x2
            if last:
                high, low = (high * SCALE).astype(BF16), (low * SCALE).astype(BF16)
            dq_ref[pl.ds(qh, HALF), cols] = high
            dq_ref[pl.ds(ql, HALF), cols] = low
        dv_a = add(dv_a, dot(cat(g_a, 1), cat(p_a, 0)))
        dv_b = add(dv_b, dot(cat(g_b, 1), cat(p_b, 0)))
        dk_a = add(dk_a, dot(cat(q_a, 1), cat(d_a, 0)))
        dk_b = add(dk_b, dot(cat(q_b, 1), cat(d_b, 0)))
    dk_a, dk_b = dk_a * SCALE, dk_b * SCALE
    dkv_ref[pl.ds(kl, HALF), :] = (dk_a + in_low * dk_b).T.astype(BF16)
    dkv_ref[pl.ds(kh, HALF), :] = (in_high * dk_b).T.astype(BF16)
    dkv_ref[pl.ds(pl.multiple_of(T + kl, HALF), HALF), :] = (dv_a + in_low * dv_b).T.astype(BF16)
    dkv_ref[pl.ds(pl.multiple_of(T + kh, HALF), HALF), :] = (in_high * dv_b).T.astype(BF16)


def vmem():
    return pl.BlockSpec(memory_space=pltpu.VMEM)


def cost(quadrants, size):
    return pl.CostEstimate(
        flops=quadrants * H * 20 * HALF * HALF * D,
        bytes_accessed=size,
        transcendentals=quadrants * H * HALF * HALF,
    )


def hbm():
    return pl.BlockSpec(memory_space=pltpu.HBM)


def pack(k, v, positions):
    return pl.pallas_call(
        pack_kernel,
        in_specs=[hbm()] * 3,
        out_specs=vmem(),
        out_shape=jax.ShapeDtypeStruct((2 * T + IDS, D), BF16),
        scratch_shapes=[pltpu.SMEM(positions.shape, jnp.int32), pltpu.SemaphoreType.DMA((3,))],
        name="pack",
    )(k, v, positions)


def own_block(q, g, o, l, message):
    return pl.pallas_call(
        own_kernel,
        in_specs=[hbm()] * 4 + [vmem()],
        out_specs=[vmem()] * 5,
        out_shape=[
            jax.ShapeDtypeStruct((T, H * D), F32),
            jax.ShapeDtypeStruct((2 * T, D), F32),
            jax.ShapeDtypeStruct((2 * H, T), F32),
            jax.ShapeDtypeStruct((T, H * D), BF16),
            jax.ShapeDtypeStruct((T, H * D), BF16),
        ],
        scratch_shapes=[
            pltpu.VMEM((T, H * D), BF16),
            pltpu.VMEM((H, T), F32),
            pltpu.VMEM((T, 2 * H), F32),
            pltpu.SemaphoreType.DMA((H // GROUP, 4)),
        ],
        compiler_params=pltpu.CompilerParams(vmem_limit_bytes=24 << 20),
        cost_estimate=cost(3, 6 << 20),
        name="own_block",
    )(q, g, o, l, message)


def other_block(last, q, g, stat, message, theirs, part):
    return pl.pallas_call(
        functools.partial(other_kernel, last),
        in_specs=[vmem()] * 6,
        out_specs=[vmem()] * 2,
        out_shape=[
            jax.ShapeDtypeStruct((T, H * D), BF16 if last else F32),
            jax.ShapeDtypeStruct((2 * T, D), BF16),
        ],
        scratch_shapes=[pltpu.VMEM((T, 2 * H), F32)],
        compiler_params=pltpu.CompilerParams(vmem_limit_bytes=24 << 20),
        cost_estimate=cost(2, 6 << 20),
        name="other_block",
    )(q, g, stat, message, theirs, part)


def passed_along(value, steps):
    count = lax.axis_size("blk")
    pairs = [(source, (source + steps) % count) for source in range(count)]
    return lax.ppermute(value, "blk", pairs)


def swapped(value):
    count = lax.axis_size("blk")
    return lax.ppermute(value, "blk", [(source, source ^ 1) for source in range(count)])


def on_device(q, k, v, o, g, log_total, positions):
    q, k, v, o, g, log_total, positions = (
        pltpu.with_memory_space_constraint(x, pltpu.HBM) for x in (q, k, v, o, g, log_total, positions)
    )
    message = pack(k, v, positions)
    two = passed_along(message, 2)
    dq, dkv, stat, q, g = own_block(q, g, o, log_total, message)
    two, dq = lax.optimization_barrier((two, dq))
    one = swapped(jnp.where(lax.axis_index("blk") % 2 == 0, message, two))
    dq, dkv_two = other_block(False, q, g, stat, message, two, dq)
    back_two = passed_along(dkv_two, -2)
    dq, dkv_one = other_block(True, q, g, stat, message, one, dq)
    back_one = passed_along(dkv_one, -1)
    total = (dkv + back_two.astype(F32) + back_one.astype(F32)).astype(BF16)
    return dq, total[:T], total[T:]


def solution(mesh):
    in_specs = (
        P("blk", "tp"),
        P("blk", "tp"),
        P("blk", "tp"),
        P("blk", "tp"),
        P("blk", "tp"),
        P("tp", "blk"),
        P(("blk", "tp")),
    )
    out_specs = (P("blk", "tp"), P("blk", "tp"), P("blk", "tp"))
    return jax.shard_map(
        on_device, mesh=mesh, in_specs=in_specs, out_specs=out_specs, check_vma=False
    )
```

```python
import functools
import math

import jax
import jax.numpy as jnp
from jax import lax
from jax.experimental import pallas as pl
from jax.experimental.pallas import tpu as pltpu
from jax.sharding import PartitionSpec as P

D = 128
H = 8
T = 512
HALF = T // 2
PIECES = 64
IDS = 16
GROUP = 4
SCALE = 1.0 / math.sqrt(D)
LOG2E = math.log2(math.e)
SCORE_SCALE = SCALE * LOG2E
F32 = jnp.float32
BF16 = jnp.bfloat16


def dot(a, b):
    return lax.dot_general(a, b, (((1,), (0,)), ((), ())), preferred_element_type=F32)


def dot_t(a, b):
    return lax.dot_general(a, b, (((1,), (1,)), ((), ())), preferred_element_type=F32)


def cat(parts, axis):
    return parts[0] if len(parts) == 1 else jnp.concatenate(parts, axis)


def products(parts, matrix):
    whole = dot(cat(parts, 0), matrix)
    return [whole[n * HALF : (n + 1) * HALF, :] for n in range(len(parts))]


def weights_of(scores, grads, log_total, row_dot, mask):
    p = jnp.exp2(scores * SCORE_SCALE - log_total)
    if mask is not None:
        p = jnp.where(mask, p, 0.0)
    ds = p * (grads - row_dot)
    return p.astype(BF16), ds.astype(BF16)


def piece_of(message):
    return jnp.max(message[T:, :].astype(F32)).astype(jnp.int32)


def low_row(first):
    return pl.multiple_of(jnp.where(first < PIECES // 2, 0, HALF), HALF)


def low_piece(first):
    return jnp.minimum(first, PIECES - 1 - first)


def pack_kernel(k_hbm, v_hbm, pos_hbm, low, high, pos, k_ref, v_ref, sems):
    copies = [
        pltpu.make_async_copy(source, target, sems.at[i])
        for i, (source, target) in enumerate(((pos_hbm, pos), (k_hbm, k_ref), (v_hbm, v_ref)))
    ]
    for copy in copies:
        copy.start()
    copies[0].wait()
    piece = pos[0] // HALF
    in_first = lax.axis_index("tp") < lax.axis_size("tp") // 2
    first = jnp.where(in_first, piece, PIECES - 1 - piece)
    low[T:, :] = jnp.full((IDS, D), first.astype(F32), F32).astype(BF16)
    ql = low_row(first)
    qh = pl.multiple_of(HALF - ql, HALF)
    for copy, source, at in ((copies[1], k_ref, 0), (copies[2], v_ref, HALF)):
        copy.wait()
        low[at : at + HALF, :] = source[pl.ds(ql, HALF), :]
        high[at : at + HALF, :] = source[pl.ds(qh, HALF), :]


def transposed_stat(stat_ref, stat_t):
    stat_t[...] = stat_ref[...].T


def stat_of(stat_t, rows, h):
    return stat_t[pl.ds(rows, HALF), h : h + 1], stat_t[pl.ds(rows, HALF), H + h : H + h + 1]


def stat_kernel(q_hbm, g_hbm, o_hbm, l_hbm, message, q_ref, g_ref, stat_ref, o_ref, l_ref, sems):
    load_l = pltpu.make_async_copy(l_hbm, l_ref, sems.at[0, 2])
    load_q = pltpu.make_async_copy(q_hbm, q_ref, sems.at[1, 2])
    loads = []
    for n, h0 in enumerate(range(0, H, GROUP)):
        cols = pl.ds(h0 * D, GROUP * D)
        loads.append(
            [
                pltpu.make_async_copy(source.at[:, cols], target.at[:, cols], sems.at[n, i])
                for i, (source, target) in enumerate(((g_hbm, g_ref), (o_hbm, o_ref)))
            ]
        )
        for load in loads[n]:
            load.start()
    load_l.start()
    load_q.start()
    rows = lax.broadcasted_iota(jnp.int32, (H, 2 * D), 0)
    row_dot = jnp.zeros((H, T), F32)
    for n, h0 in enumerate(range(0, H, GROUP)):
        for load in loads[n]:
            load.wait()
        for h in range(h0, h0 + GROUP):
            cols = slice(h * D, (h + 1) * D)
            prod = g_ref[:, cols].astype(F32) * o_ref[:, cols].astype(F32)
            top = prod.astype(BF16)
            rest = (prod - top.astype(F32)).astype(BF16)
            pick = jnp.where(rows == h, 1.0, 0.0).astype(BF16)
            row_dot += dot_t(pick, jnp.concatenate([top, rest], 1))
    load_l.wait()
    stat_ref[0:H, :] = l_ref[...] * LOG2E
    stat_ref[H : 2 * H, :] = row_dot
    stat_ref[2 * H :, :] = jnp.full((H, T), piece_of(message).astype(F32), F32)
    load_q.wait()


def own_kernel(q_ref, g_ref, stat_ref, low_ref, high_ref, keep_ref, keep_h, x_low, x_high, dq_ref, low_total, high_total, stat_t):
    transposed_stat(stat_ref, stat_t)
    ql = low_row(piece_of(low_ref))
    qh = pl.multiple_of(HALF - ql, HALF)
    mask = lax.broadcasted_iota(jnp.int32, (HALF, HALF), 1) <= lax.broadcasted_iota(
        jnp.int32, (HALF, HALF), 0
    )
    kl, vl = low_ref[:HALF, :], low_ref[HALF:T, :]
    kh, vh = high_ref[:HALF, :], high_ref[HALF:, :]
    sums = None
    for h0 in (0, GROUP):
        heads = [slice(h * D, (h + 1) * D) for h in range(h0, h0 + GROUP)]
        q0, q1 = ([q_ref[pl.ds(rows, HALF), cols] for cols in heads] for rows in (ql, qh))
        g0, g1 = ([g_ref[pl.ds(rows, HALF), cols] for cols in heads] for rows in (ql, qh))
        scores_l, grads_l = products(q0 + q1, kl.T), products(g0 + g1, vl.T)
        scores_h, grads_h = products(q1, kh.T), products(g1, vh.T)
        p_l, d_l, p_h, d_h = [], [], [], []
        for n in range(2 * GROUP):
            rows, masked = (ql, mask) if n < GROUP else (qh, None)
            stat = stat_of(stat_t, rows, h0 + n % GROUP)
            p, d = weights_of(scores_l[n], grads_l[n], *stat, masked)
            p_l, d_l = p_l + [p], d_l + [d]
        for n in range(GROUP):
            p, d = weights_of(scores_h[n], grads_h[n], *stat_of(stat_t, qh, h0 + n), mask)
            p_h, d_h = p_h + [p], d_h + [d]
        lows = products(d_l[:GROUP], kl)
        highs = products(
            [jnp.concatenate([d_l[GROUP + n], d_h[n]], 1) for n in range(GROUP)],
            jnp.concatenate([kl, kh], 0),
        )
        for n, cols in enumerate(heads):
            dq_ref[pl.ds(ql, HALF), cols] = keep_ref[pl.ds(ql, HALF), cols].astype(F32) + lows[n]
            kept = keep_ref[pl.ds(qh, HALF), cols].astype(F32) + keep_h[:, cols].astype(F32)
            dq_ref[pl.ds(qh, HALF), cols] = kept + highs[n]
        g0_t, g1_t = cat([g.T for g in g0], 1), cat([g.T for g in g1], 1)
        q0_t, q1_t = cat([q.T for q in q0], 1), cat([q.T for q in q1], 1)
        dv_l, dv_h = dot(cat([g0_t, g1_t], 1), cat(p_l, 0)), dot(g1_t, cat(p_h, 0))
        dk_l, dk_h = dot(cat([q0_t, q1_t], 1), cat(d_l, 0)), dot(q1_t, cat(d_h, 0))
        part = (dk_l, dv_l, dk_h, dv_h)
        sums = part if sums is None else tuple(x + y for x, y in zip(sums, part))
    dk_l, dv_l, dk_h, dv_h = sums
    even = is_even()
    for total, more, dk, dv in ((low_total, x_low, dk_l, dv_l), (high_total, x_high, dk_h, dv_h)):
        total[:HALF, :] = (dk * SCALE).T + jnp.where(even, more[:HALF, :], 0.0)
        total[HALF:, :] = dv.T + jnp.where(even, more[HALF:, :], 0.0)


class Queries:

    def __init__(self, q_ref, g_ref, stat_ref, theirs_low, stat_t):
        transposed_stat(stat_ref, stat_t)
        self.q_ref, self.g_ref, self.stat_t = q_ref, g_ref, stat_t
        first = jnp.max(stat_ref[2 * H :, :]).astype(jnp.int32)
        self.low = low_row(first)
        self.high = pl.multiple_of(HALF - self.low, HALF)
        self.lows = low_piece(first) > low_piece(piece_of(theirs_low))

    def quadrant(self, rows, keys, dq_ref, at):
        k, v = keys[:HALF, :], keys[HALF:T, :]
        k_t, v_t = k.T, v.T
        heads = [slice(h * D, (h + 1) * D) for h in range(H)]
        qs = [self.q_ref[pl.ds(rows, HALF), cols] for cols in heads]
        gs = [self.g_ref[pl.ds(rows, HALF), cols] for cols in heads]
        scores, grads = products(qs, k_t), products(gs, v_t)
        ps, ds = [], []
        for h in range(H):
            p, d = weights_of(scores[h], grads[h], *stat_of(self.stat_t, rows, h), None)
            ps, ds = ps + [p], ds + [d]
        for h, x in enumerate(products(ds, k)):
            dq_ref[pl.ds(at, HALF), heads[h]] = x.astype(BF16)
        dv = dot(cat([g.T for g in gs], 1), cat(ps, 0))
        dk = dot(cat([q.T for q in qs], 1), cat(ds, 0))
        return (dk * SCALE).T, dv.T

    def low_keys(self, keys, dq_ref, total):
        dk, dv = self.quadrant(self.high, keys, dq_ref, self.high)
        total[:HALF, :] = dk
        total[HALF:, :] = dv

        @pl.when(self.lows)
        def _():
            dk, dv = self.quadrant(self.low, keys, dq_ref, self.low)
            total[:HALF, :] += dk
            total[HALF:, :] += dv

        @pl.when(jnp.logical_not(self.lows))
        def _():
            dq_ref[pl.ds(self.low, HALF), :] = jnp.zeros((HALF, H * D), BF16)

    def high_keys(self, keys, dq_ref, total, adds):
        @pl.when(jnp.logical_not(self.lows))
        def _():
            dk, dv = self.quadrant(self.high, keys, dq_ref, 0)
            if adds:
                total[:HALF, :] += dk
                total[HALF:, :] += dv
            else:
                total[:HALF, :] = dk
                total[HALF:, :] = dv

        @pl.when(self.lows)
        def _():
            dq_ref[...] = jnp.zeros((HALF, H * D), BF16)
            if not adds:
                total[...] = jnp.zeros((T, D), F32)


def is_even():
    return lax.axis_index("blk") % 2 == 0


def first_kernel(q_ref, g_ref, stat_ref, theirs_low, dq_ref, low_total, stat_t):
    queries = Queries(q_ref, g_ref, stat_ref, theirs_low, stat_t)
    queries.low_keys(theirs_low, dq_ref, low_total)


def second_kernel(q2_ref, g2_ref, stat2_ref, own_low, own_high, theirs_low, dq_ref, dq_h, x_low, x_high, stat_t):
    even = is_even()

    @pl.when(even)
    def _():
        queries = Queries(q2_ref, g2_ref, stat2_ref, own_low, stat_t)
        queries.low_keys(own_low, dq_ref, x_low)
        queries.high_keys(own_high, dq_h, x_high, False)

    @pl.when(jnp.logical_not(even))
    def _():
        Queries(q2_ref, g2_ref, stat2_ref, theirs_low, stat_t).low_keys(theirs_low, dq_ref, x_low)


def send_whole(stat2_ref, dq_ref, dq_h, out_ref):
    high = pl.multiple_of(HALF - low_row(jnp.max(stat2_ref[2 * H :, :]).astype(jnp.int32)), HALF)
    low = pl.multiple_of(HALF - high, HALF)
    total = dq_ref[pl.ds(high, HALF), :].astype(F32) + dq_h[...].astype(F32)
    out_ref[pl.ds(high, HALF), :] = total.astype(BF16)
    out_ref[pl.ds(low, HALF), :] = dq_ref[pl.ds(low, HALF), :]


def third_kernel(q_ref, g_ref, stat_ref, q2_ref, g2_ref, stat2_ref, theirs_low, theirs_high, low_total, x_low, x_dq, x_dq_h, keep_h, send, back, high_total, dq_h, stat_t):
    even = is_even()
    queries = Queries(q_ref, g_ref, stat_ref, theirs_low, stat_t)
    queries.high_keys(theirs_high, keep_h, high_total, False)

    @pl.when(even)
    def _():
        send_whole(stat2_ref, x_dq, x_dq_h, send)
        back[:T, :] = low_total[...].astype(BF16)

    @pl.when(jnp.logical_not(even))
    def _():
        others = Queries(q2_ref, g2_ref, stat2_ref, theirs_low, stat_t)
        others.high_keys(theirs_high, dq_h, high_total, True)
        send_whole(stat2_ref, x_dq, dq_h, send)
        back[:T, :] = (low_total[...] + x_low[...]).astype(BF16)

    back[T:, :] = high_total[...].astype(BF16)


def query_kernel(dq_ref, got_ref, out_ref):
    out_ref[...] = ((dq_ref[...] + got_ref[...].astype(F32)) * SCALE).astype(BF16)


def key_kernel(own_low, low_total, high_total, got_ref, dk_ref, dv_ref):
    ql = low_row(piece_of(own_low))
    qh = pl.multiple_of(HALF - ql, HALF)
    for total, rows, at in ((low_total, ql, 0), (high_total, qh, T)):
        for out, n in ((dk_ref, 0), (dv_ref, HALF)):
            got = got_ref[at + n : at + n + HALF, :].astype(F32)
            out[pl.ds(rows, HALF), :] = (total[n : n + HALF, :] + got).astype(BF16)


def vmem():
    return pl.BlockSpec(memory_space=pltpu.VMEM)


def cost(quadrants, size):
    return pl.CostEstimate(
        flops=int(quadrants * H * 10 * HALF * HALF * D),
        bytes_accessed=size,
        transcendentals=int(quadrants * H * HALF * HALF),
    )


def hbm():
    return pl.BlockSpec(memory_space=pltpu.HBM)


def pack(k, v, positions):
    return pl.pallas_call(
        pack_kernel,
        in_specs=[hbm()] * 3,
        out_specs=vmem(),
        out_shape=jax.ShapeDtypeStruct((2 * T + IDS, D), BF16),
        scratch_shapes=[pltpu.SMEM(positions.shape, jnp.int32), pltpu.SemaphoreType.DMA((3,))],
        name="pack",
    )(k, v, positions)


def hbm():
    return pl.BlockSpec(memory_space=pltpu.HBM)


def in_vmem(value):
    return pltpu.with_memory_space_constraint(value, pltpu.VMEM)


def array(shape, dtype):
    return jax.ShapeDtypeStruct(shape, dtype)


def call(kernel, name, ins, outs, scratch=(), quadrants=0, from_hbm=0):
    size = sum(x.size * x.dtype.itemsize for x in list(ins) + list(outs))
    return pl.pallas_call(
        kernel,
        in_specs=[hbm()] * from_hbm + [vmem()] * (len(ins) - from_hbm),
        out_specs=[vmem()] * len(outs),
        out_shape=list(outs),
        scratch_shapes=list(scratch),
        compiler_params=pltpu.CompilerParams(vmem_limit_bytes=24 << 20),
        cost_estimate=cost(quadrants, size),
        name=name,
    )(*ins)


def passed_along(value, steps):
    count = lax.axis_size("blk")
    pairs = [(source, (source + steps) % count) for source in range(count)]
    return lax.ppermute(value, "blk", pairs)


def swapped(value):
    count = lax.axis_size("blk")
    return lax.ppermute(value, "blk", [(source, source ^ 1) for source in range(count)])


def on_device(q_in, k, v, o, g_in, log_total, positions):
    q_in, k, v, o, g_in, log_total, positions = (
        pltpu.with_memory_space_constraint(x, pltpu.HBM)
        for x in (q_in, k, v, o, g_in, log_total, positions)
    )
    rows, half_rows = array((T, H * D), BF16), array((HALF, H * D), BF16)
    stat_t = pltpu.VMEM((T, 3 * H), F32)
    terms, half_terms = array((2 * T, D), F32), array((T, D), F32)
    low, high = call(
        pack_kernel,
        "pack",
        (k, v, positions),
        (array((T + IDS, D), BF16), array((T, D), BF16)),
        (
            pltpu.SMEM(positions.shape, jnp.int32),
            pltpu.VMEM((T, D), BF16),
            pltpu.VMEM((T, D), BF16),
            pltpu.SemaphoreType.DMA((3,)),
        ),
        from_hbm=3,
    )
    theirs_low = in_vmem(passed_along(low, 2))
    low, q_swap, g_swap = lax.optimization_barrier((low, q_in, g_in))
    q2, g2 = in_vmem(swapped(q_swap)), in_vmem(swapped(g_swap))
    q, g, stat = call(
        stat_kernel,
        "stat",
        (q_in, g_in, o, log_total, low),
        (rows, rows, array((3 * H, T), F32)),
        (pltpu.VMEM((T, H * D), BF16), pltpu.VMEM((H, T), F32), pltpu.SemaphoreType.DMA((2, 3))),
        from_hbm=4,
    )
    high, stat = lax.optimization_barrier((high, stat))
    theirs_high = in_vmem(passed_along(high, 2))
    stat2 = in_vmem(swapped(stat))
    keep, low_total = call(
        first_kernel,
        "first",
        (q, g, stat, theirs_low),
        (rows, half_terms),
        (stat_t,),
        quadrants=1.5,
    )
    x_dq, x_dq_h, x_low, x_high = call(
        second_kernel,
        "second",
        (q2, g2, stat2, low, high, theirs_low),
        (rows, half_rows, half_terms, half_terms),
        (stat_t,),
        quadrants=2,
    )
    theirs_high, x_dq = lax.optimization_barrier((theirs_high, x_dq))
    keep_h, send, message_back = call(
        third_kernel,
        "third",
        (q, g, stat, q2, g2, stat2, theirs_low, theirs_high, low_total, x_low, x_dq, x_dq_h),
        (half_rows, rows, array((2 * T, D), BF16)),
        (pltpu.VMEM((T, D), F32), pltpu.VMEM((HALF, H * D), BF16), stat_t),
        quadrants=0.5,
    )
    back = passed_along(message_back, -2)
    got = in_vmem(swapped(send))
    dq, own_low, own_high = call(
        own_kernel,
        "own",
        (q, g, stat, low, high, keep, keep_h, x_low, x_high),
        (array((T, H * D), F32), half_terms, half_terms),
        (stat_t,),
        quadrants=3,
    )
    (dq,) = call(query_kernel, "query_sum", (dq, got), (rows,))
    back, dq = lax.optimization_barrier((back, dq))
    dk, dv = call(
        key_kernel, "key_sum", (low, own_low, own_high, back), (array((T, D), BF16),) * 2
    )
    return dq, dk, dv


def solution(mesh):
    in_specs = (
        P("blk", "tp"),
        P("blk", "tp"),
        P("blk", "tp"),
        P("blk", "tp"),
        P("blk", "tp"),
        P("tp", "blk"),
        P(("blk", "tp")),
    )
    out_specs = (P("blk", "tp"), P("blk", "tp"), P("blk", "tp"))
    return jax.shard_map(
        on_device, mesh=mesh, in_specs=in_specs, out_specs=out_specs, check_vma=False
    )
```

```python
import functools
import math

import jax
import jax.numpy as jnp
from jax import lax
from jax.experimental import pallas as pl
from jax.experimental.pallas import tpu as pltpu
from jax.sharding import PartitionSpec as P

D = 128
H = 8
T = 512
HALF = T // 2
PIECES = 64
IDS = 16
GROUP = 4
SCALE = 1.0 / math.sqrt(D)
LOG2E = math.log2(math.e)
SCORE_SCALE = SCALE * LOG2E
F32 = jnp.float32
BF16 = jnp.bfloat16


def dot(a, b):
    return lax.dot_general(a, b, (((1,), (0,)), ((), ())), preferred_element_type=F32)


def dot_t(a, b):
    return lax.dot_general(a, b, (((1,), (1,)), ((), ())), preferred_element_type=F32)


def cat(parts, axis):
    return parts[0] if len(parts) == 1 else jnp.concatenate(parts, axis)


def products(parts, matrix):
    whole = dot(cat(parts, 0), matrix)
    return [whole[n * HALF : (n + 1) * HALF, :] for n in range(len(parts))]


def weights_of(scores, grads, log_total, row_dot, mask):
    p = jnp.exp2(scores * SCORE_SCALE - log_total)
    if mask is not None:
        p = jnp.where(mask, p, 0.0)
    ds = p * (grads - row_dot)
    return p.astype(BF16), ds.astype(BF16)


def piece_of(message):
    return jnp.max(message[T:, :].astype(F32)).astype(jnp.int32)


def low_row(first):
    return pl.multiple_of(jnp.where(first < PIECES // 2, 0, HALF), HALF)


def low_piece(first):
    return jnp.minimum(first, PIECES - 1 - first)


def pack_kernel(k_hbm, v_hbm, pos_hbm, low, high, pos, k_ref, v_ref, sems):
    copies = [
        pltpu.make_async_copy(source, target, sems.at[i])
        for i, (source, target) in enumerate(((pos_hbm, pos), (k_hbm, k_ref), (v_hbm, v_ref)))
    ]
    for copy in copies:
        copy.start()
    copies[0].wait()
    piece = pos[0] // HALF
    in_first = lax.axis_index("tp") < lax.axis_size("tp") // 2
    first = jnp.where(in_first, piece, PIECES - 1 - piece)
    low[T:, :] = jnp.full((IDS, D), first.astype(F32), F32).astype(BF16)
    ql = low_row(first)
    qh = pl.multiple_of(HALF - ql, HALF)
    for copy, source, at in ((copies[1], k_ref, 0), (copies[2], v_ref, HALF)):
        copy.wait()
        low[at : at + HALF, :] = source[pl.ds(ql, HALF), :]
        high[at : at + HALF, :] = source[pl.ds(qh, HALF), :]


def transposed_stat(stat_ref, stat_t):
    stat_t[...] = stat_ref[...].T


def stat_of(stat_t, rows, h):
    return stat_t[pl.ds(rows, HALF), h : h + 1], stat_t[pl.ds(rows, HALF), H + h : H + h + 1]


def stat_kernel(q_hbm, g_hbm, o_hbm, l_hbm, message, q_ref, g_ref, stat_ref, o_ref, l_ref, sems):
    load_l = pltpu.make_async_copy(l_hbm, l_ref, sems.at[0, 2])
    load_q = pltpu.make_async_copy(q_hbm, q_ref, sems.at[1, 2])
    loads = []
    for n, h0 in enumerate(range(0, H, GROUP)):
        cols = pl.ds(h0 * D, GROUP * D)
        loads.append(
            [
                pltpu.make_async_copy(source.at[:, cols], target.at[:, cols], sems.at[n, i])
                for i, (source, target) in enumerate(((g_hbm, g_ref), (o_hbm, o_ref)))
            ]
        )
        for load in loads[n]:
            load.start()
    load_l.start()
    load_q.start()
    rows = lax.broadcasted_iota(jnp.int32, (H, 2 * D), 0)
    row_dot = jnp.zeros((H, T), F32)
    for n, h0 in enumerate(range(0, H, GROUP)):
        for load in loads[n]:
            load.wait()
        for h in range(h0, h0 + GROUP):
            cols = slice(h * D, (h + 1) * D)
            prod = g_ref[:, cols].astype(F32) * o_ref[:, cols].astype(F32)
            top = prod.astype(BF16)
            rest = (prod - top.astype(F32)).astype(BF16)
            pick = jnp.where(rows == h, 1.0, 0.0).astype(BF16)
            row_dot += dot_t(pick, jnp.concatenate([top, rest], 1))
    load_l.wait()
    stat_ref[0:H, :] = l_ref[...] * LOG2E
    stat_ref[H : 2 * H, :] = row_dot
    stat_ref[2 * H :, :] = jnp.full((H, T), piece_of(message).astype(F32), F32)
    load_q.wait()


def own_kernel(q_ref, g_ref, stat_ref, low_ref, high_ref, keep_ref, x_low, x_high, dq_ref, low_total, high_total, stat_t):
    transposed_stat(stat_ref, stat_t)
    ql = low_row(piece_of(low_ref))
    qh = pl.multiple_of(HALF - ql, HALF)
    mask = lax.broadcasted_iota(jnp.int32, (HALF, HALF), 1) <= lax.broadcasted_iota(
        jnp.int32, (HALF, HALF), 0
    )
    kl, vl = low_ref[:HALF, :], low_ref[HALF:T, :]
    kh, vh = high_ref[:HALF, :], high_ref[HALF:, :]
    sums = None
    for h0 in (0, GROUP):
        heads = [slice(h * D, (h + 1) * D) for h in range(h0, h0 + GROUP)]
        q0, q1 = ([q_ref[pl.ds(rows, HALF), cols] for cols in heads] for rows in (ql, qh))
        g0, g1 = ([g_ref[pl.ds(rows, HALF), cols] for cols in heads] for rows in (ql, qh))
        scores_l, grads_l = products(q0 + q1, kl.T), products(g0 + g1, vl.T)
        scores_h, grads_h = products(q1, kh.T), products(g1, vh.T)
        p_l, d_l, p_h, d_h = [], [], [], []
        for n in range(2 * GROUP):
            rows, masked = (ql, mask) if n < GROUP else (qh, None)
            stat = stat_of(stat_t, rows, h0 + n % GROUP)
            p, d = weights_of(scores_l[n], grads_l[n], *stat, masked)
            p_l, d_l = p_l + [p], d_l + [d]
        for n in range(GROUP):
            p, d = weights_of(scores_h[n], grads_h[n], *stat_of(stat_t, qh, h0 + n), mask)
            p_h, d_h = p_h + [p], d_h + [d]
        lows = products(d_l[:GROUP], kl)
        highs = products(
            [jnp.concatenate([d_l[GROUP + n], d_h[n]], 1) for n in range(GROUP)],
            jnp.concatenate([kl, kh], 0),
        )
        for n, cols in enumerate(heads):
            dq_ref[pl.ds(ql, HALF), cols] = keep_ref[pl.ds(ql, HALF), cols].astype(F32) + lows[n]
            kept = keep_ref[pl.ds(qh, HALF), cols].astype(F32)
            dq_ref[pl.ds(qh, HALF), cols] = kept + highs[n]
        g0_t, g1_t = cat([g.T for g in g0], 1), cat([g.T for g in g1], 1)
        q0_t, q1_t = cat([q.T for q in q0], 1), cat([q.T for q in q1], 1)
        dv_l, dv_h = dot(cat([g0_t, g1_t], 1), cat(p_l, 0)), dot(g1_t, cat(p_h, 0))
        dk_l, dk_h = dot(cat([q0_t, q1_t], 1), cat(d_l, 0)), dot(q1_t, cat(d_h, 0))
        part = (dk_l, dv_l, dk_h, dv_h)
        sums = part if sums is None else tuple(x + y for x, y in zip(sums, part))
    dk_l, dv_l, dk_h, dv_h = sums
    even = is_even()
    for total, more, dk, dv in ((low_total, x_low, dk_l, dv_l), (high_total, x_high, dk_h, dv_h)):
        total[:HALF, :] = (dk * SCALE).T + jnp.where(even, more[:HALF, :], 0.0)
        total[HALF:, :] = dv.T + jnp.where(even, more[HALF:, :], 0.0)


class Queries:

    def __init__(self, q_ref, g_ref, stat_ref, theirs_low, stat_t):
        transposed_stat(stat_ref, stat_t)
        self.q_ref, self.g_ref, self.stat_t = q_ref, g_ref, stat_t
        first = jnp.max(stat_ref[2 * H :, :]).astype(jnp.int32)
        self.low = low_row(first)
        self.high = pl.multiple_of(HALF - self.low, HALF)
        self.lows = low_piece(first) > low_piece(piece_of(theirs_low))

    def quadrants(self, runs, keys, dq_ref, adds):
        k, v = keys[:HALF, :], keys[HALF:T, :]
        k_t, v_t = k.T, v.T
        heads = [slice(h * D, (h + 1) * D) for h in range(H)]
        q_t, g_t, ps, ds = [], [], [], []
        for rows in runs:
            qs = [self.q_ref[pl.ds(rows, HALF), cols] for cols in heads]
            gs = [self.g_ref[pl.ds(rows, HALF), cols] for cols in heads]
            scores, grads = products(qs, k_t), products(gs, v_t)
            for h in range(H):
                p, d = weights_of(scores[h], grads[h], *stat_of(self.stat_t, rows, h), None)
                ps, ds = ps + [p], ds + [d]
            q_t, g_t = q_t + [q.T for q in qs], g_t + [g.T for g in gs]
            for cols, x in zip(heads, products(ds[-H:], k)):
                if adds:
                    x += dq_ref[pl.ds(rows, HALF), cols].astype(F32)
                dq_ref[pl.ds(rows, HALF), cols] = x.astype(BF16)
        dv = dot(cat(g_t, 1), cat(ps, 0))
        dk = dot(cat(q_t, 1), cat(ds, 0))
        return (dk * SCALE).T, dv.T

    def low_keys(self, keys, dq_ref, total):
        @pl.when(self.lows)
        def _():
            dk, dv = self.quadrants((self.high, self.low), keys, dq_ref, False)
            total[:HALF, :] = dk
            total[HALF:, :] = dv

        @pl.when(jnp.logical_not(self.lows))
        def _():
            dq_ref[pl.ds(self.low, HALF), :] = jnp.zeros((HALF, H * D), BF16)
            dk, dv = self.quadrants((self.high,), keys, dq_ref, False)
            total[:HALF, :] = dk
            total[HALF:, :] = dv

    def high_keys(self, keys, dq_ref, total, adds):
        @pl.when(jnp.logical_not(self.lows))
        def _():
            dk, dv = self.quadrants((self.high,), keys, dq_ref, True)
            if adds:
                dk, dv = dk + total[:HALF, :], dv + total[HALF:, :]
            total[:HALF, :] = dk
            total[HALF:, :] = dv

        if not adds:

            @pl.when(self.lows)
            def _():
                total[...] = jnp.zeros((T, D), F32)


def is_even():
    return lax.axis_index("blk") % 2 == 0


def first_kernel(q_ref, g_ref, stat_ref, theirs_low, dq_ref, low_total, stat_t):
    queries = Queries(q_ref, g_ref, stat_ref, theirs_low, stat_t)
    queries.low_keys(theirs_low, dq_ref, low_total)


def second_kernel(q2_ref, g2_ref, stat2_ref, own_low, own_high, theirs_low, dq_ref, x_low, x_high, stat_t):
    even = is_even()

    @pl.when(even)
    def _():
        queries = Queries(q2_ref, g2_ref, stat2_ref, own_low, stat_t)
        queries.low_keys(own_low, dq_ref, x_low)
        queries.high_keys(own_high, dq_ref, x_high, False)

    @pl.when(jnp.logical_not(even))
    def _():
        Queries(q2_ref, g2_ref, stat2_ref, theirs_low, stat_t).low_keys(theirs_low, dq_ref, x_low)


def third_kernel(q_ref, g_ref, stat_ref, q2_ref, g2_ref, stat2_ref, theirs_low, theirs_high, low_total, x_low, _, __, keep, send, back, high_total, stat_t):
    even = is_even()
    Queries(q_ref, g_ref, stat_ref, theirs_low, stat_t).high_keys(
        theirs_high, keep, high_total, False
    )

    @pl.when(even)
    def _():
        back[:T, :] = low_total[...].astype(BF16)

    @pl.when(jnp.logical_not(even))
    def _():
        back[:T, :] = (low_total[...] + x_low[...]).astype(BF16)
        others = Queries(q2_ref, g2_ref, stat2_ref, theirs_low, stat_t)
        others.high_keys(theirs_high, send, high_total, True)

    back[T:, :] = high_total[...].astype(BF16)


def query_kernel(dq_ref, got_ref, out_ref):
    out_ref[...] = ((dq_ref[...] + got_ref[...].astype(F32)) * SCALE).astype(BF16)


def key_kernel(own_low, low_total, high_total, got_ref, dk_ref, dv_ref):
    ql = low_row(piece_of(own_low))
    qh = pl.multiple_of(HALF - ql, HALF)
    for total, rows, at in ((low_total, ql, 0), (high_total, qh, T)):
        for out, n in ((dk_ref, 0), (dv_ref, HALF)):
            got = got_ref[at + n : at + n + HALF, :].astype(F32)
            out[pl.ds(rows, HALF), :] = (total[n : n + HALF, :] + got).astype(BF16)


def vmem():
    return pl.BlockSpec(memory_space=pltpu.VMEM)


def cost(quadrants, size):
    return pl.CostEstimate(
        flops=int(quadrants * H * 10 * HALF * HALF * D),
        bytes_accessed=size,
        transcendentals=int(quadrants * H * HALF * HALF),
    )


def hbm():
    return pl.BlockSpec(memory_space=pltpu.HBM)


def pack(k, v, positions):
    return pl.pallas_call(
        pack_kernel,
        in_specs=[hbm()] * 3,
        out_specs=vmem(),
        out_shape=jax.ShapeDtypeStruct((2 * T + IDS, D), BF16),
        scratch_shapes=[pltpu.SMEM(positions.shape, jnp.int32), pltpu.SemaphoreType.DMA((3,))],
        name="pack",
    )(k, v, positions)


def hbm():
    return pl.BlockSpec(memory_space=pltpu.HBM)


def in_vmem(value):
    return pltpu.with_memory_space_constraint(value, pltpu.VMEM)


def array(shape, dtype):
    return jax.ShapeDtypeStruct(shape, dtype)


def call(kernel, name, ins, outs, scratch=(), quadrants=0, from_hbm=0, aliases=None):
    size = sum(x.size * x.dtype.itemsize for x in list(ins) + list(outs))
    return pl.pallas_call(
        kernel,
        in_specs=[hbm()] * from_hbm + [vmem()] * (len(ins) - from_hbm),
        out_specs=[vmem()] * len(outs),
        out_shape=list(outs),
        scratch_shapes=list(scratch),
        input_output_aliases=aliases or {},
        compiler_params=pltpu.CompilerParams(vmem_limit_bytes=24 << 20),
        cost_estimate=cost(quadrants, size),
        name=name,
    )(*ins)


def passed_along(value, steps):
    count = lax.axis_size("blk")
    pairs = [(source, (source + steps) % count) for source in range(count)]
    return lax.ppermute(value, "blk", pairs)


def swapped(value):
    count = lax.axis_size("blk")
    return lax.ppermute(value, "blk", [(source, source ^ 1) for source in range(count)])


def on_device(q_in, k, v, o, g_in, log_total, positions):
    q_in, k, v, o, g_in, log_total, positions = (
        pltpu.with_memory_space_constraint(x, pltpu.HBM)
        for x in (q_in, k, v, o, g_in, log_total, positions)
    )
    rows = array((T, H * D), BF16)
    stat_t = pltpu.VMEM((T, 3 * H), F32)
    terms, half_terms = array((2 * T, D), F32), array((T, D), F32)
    low, high = call(
        pack_kernel,
        "pack",
        (k, v, positions),
        (array((T + IDS, D), BF16), array((T, D), BF16)),
        (
            pltpu.SMEM(positions.shape, jnp.int32),
            pltpu.VMEM((T, D), BF16),
            pltpu.VMEM((T, D), BF16),
            pltpu.SemaphoreType.DMA((3,)),
        ),
        from_hbm=3,
    )
    theirs_low = in_vmem(passed_along(low, 2))
    low, q_swap, g_swap = lax.optimization_barrier((low, q_in, g_in))
    q2, g2 = in_vmem(swapped(q_swap)), in_vmem(swapped(g_swap))
    q, g, stat = call(
        stat_kernel,
        "stat",
        (q_in, g_in, o, log_total, low),
        (rows, rows, array((3 * H, T), F32)),
        (pltpu.VMEM((T, H * D), BF16), pltpu.VMEM((H, T), F32), pltpu.SemaphoreType.DMA((2, 3))),
        quadrants=30,
        from_hbm=4,
    )
    high, stat = lax.optimization_barrier((high, stat))
    theirs_high = in_vmem(passed_along(high, 2))
    stat2 = in_vmem(swapped(stat))
    keep, low_total = call(
        first_kernel,
        "first",
        (q, g, stat, theirs_low),
        (rows, half_terms),
        (stat_t,),
        quadrants=1.5,
    )
    send, x_low, x_high = call(
        second_kernel,
        "second",
        (q2, g2, stat2, low, high, theirs_low),
        (rows, half_terms, half_terms),
        (stat_t,),
        quadrants=2,
    )
    theirs_high, send = lax.optimization_barrier((theirs_high, send))
    keep, send, message_back = call(
        third_kernel,
        "third",
        (q, g, stat, q2, g2, stat2, theirs_low, theirs_high, low_total, x_low, keep, send),
        (rows, rows, array((2 * T, D), BF16)),
        (pltpu.VMEM((T, D), F32), stat_t),
        quadrants=0.5,
        aliases={10: 0, 11: 1},
    )
    back = passed_along(message_back, -2)
    got = in_vmem(swapped(send))
    dq, own_low, own_high = call(
        own_kernel,
        "own",
        (q, g, stat, low, high, keep, x_low, x_high),
        (array((T, H * D), F32), half_terms, half_terms),
        (stat_t,),
        quadrants=60,
    )
    (dq,) = call(query_kernel, "query_sum", (dq, got), (rows,))
    back, dq = lax.optimization_barrier((back, dq))
    dk, dv = call(
        key_kernel, "key_sum", (low, own_low, own_high, back), (array((T, D), BF16),) * 2
    )
    return dq, dk, dv


def solution(mesh):
    in_specs = (
        P("blk", "tp"),
        P("blk", "tp"),
        P("blk", "tp"),
        P("blk", "tp"),
        P("blk", "tp"),
        P("tp", "blk"),
        P(("blk", "tp")),
    )
    out_specs = (P("blk", "tp"), P("blk", "tp"), P("blk", "tp"))
    return jax.shard_map(
        on_device, mesh=mesh, in_specs=in_specs, out_specs=out_specs, check_vma=False
    )
```

```python
import functools
import math

import jax
import jax.numpy as jnp
from jax import lax
from jax.experimental import pallas as pl
from jax.experimental.pallas import tpu as pltpu
from jax.sharding import PartitionSpec as P

D = 128
H = 8
T = 512
STEPS = 2
HALF = T // 2
PIECES = 64
IDS = 16
GROUP = 4
SCALE = 1.0 / math.sqrt(D)
LOG2E = math.log2(math.e)
SCORE_SCALE = SCALE * LOG2E
F32 = jnp.float32
BF16 = jnp.bfloat16


def dot(a, b):
    return lax.dot_general(a, b, (((1,), (0,)), ((), ())), preferred_element_type=F32)


def dot_t(a, b):
    return lax.dot_general(a, b, (((1,), (1,)), ((), ())), preferred_element_type=F32)


def cat(parts, axis):
    return parts[0] if len(parts) == 1 else jnp.concatenate(parts, axis)


def products(parts, matrix):
    whole = dot(cat(parts, 0), matrix)
    return [whole[n * HALF : (n + 1) * HALF, :] for n in range(len(parts))]


def weights_of(scores, grads, log_total, row_dot, mask):
    p = jnp.exp2(scores * SCORE_SCALE - log_total)
    if mask is not None:
        p = jnp.where(mask, p, 0.0)
    ds = p * (grads - row_dot)
    return p.astype(BF16), ds.astype(BF16)


def piece_of(message):
    return jnp.max(message[T:, :].astype(F32)).astype(jnp.int32)


def low_row(first):
    return pl.multiple_of(jnp.where(first < PIECES // 2, 0, HALF), HALF)


def low_piece(first):
    return jnp.minimum(first, PIECES - 1 - first)


def pack_kernel(k_hbm, v_hbm, pos_hbm, low, high, pos, k_ref, v_ref, sems):
    copies = [
        pltpu.make_async_copy(source, target, sems.at[i])
        for i, (source, target) in enumerate(((pos_hbm, pos), (k_hbm, k_ref), (v_hbm, v_ref)))
    ]
    for copy in copies:
        copy.start()
    copies[0].wait()
    piece = pos[0] // HALF
    in_first = lax.axis_index("tp") < lax.axis_size("tp") // 2
    first = jnp.where(in_first, piece, PIECES - 1 - piece)
    low[T:, :] = jnp.full((IDS, D), first.astype(F32), F32).astype(BF16)
    ql = low_row(first)
    qh = pl.multiple_of(HALF - ql, HALF)
    for copy, source, at in ((copies[1], k_ref, 0), (copies[2], v_ref, HALF)):
        copy.wait()
        low[at : at + HALF, :] = source[pl.ds(ql, HALF), :]
        high[at : at + HALF, :] = source[pl.ds(qh, HALF), :]


def transposed_stat(stat_ref, stat_t):
    stat_t[...] = stat_ref[...].T


def stat_of(stat_t, rows, h):
    return stat_t[pl.ds(rows, HALF), h : h + 1], stat_t[pl.ds(rows, HALF), H + h : H + h + 1]


def stat_kernel(q_hbm, g_hbm, o_hbm, l_hbm, message, q_ref, g_ref, stat_ref, o_ref, l_ref, sems):
    load_l = pltpu.make_async_copy(l_hbm, l_ref, sems.at[0, 2])
    load_q = pltpu.make_async_copy(q_hbm, q_ref, sems.at[1, 2])
    loads = []
    for n, h0 in enumerate(range(0, H, GROUP)):
        cols = pl.ds(h0 * D, GROUP * D)
        loads.append(
            [
                pltpu.make_async_copy(source.at[:, cols], target.at[:, cols], sems.at[n, i])
                for i, (source, target) in enumerate(((g_hbm, g_ref), (o_hbm, o_ref)))
            ]
        )
        for load in loads[n]:
            load.start()
    load_l.start()
    load_q.start()
    rows = lax.broadcasted_iota(jnp.int32, (H, 2 * D), 0)
    row_dot = jnp.zeros((H, T), F32)
    for n, h0 in enumerate(range(0, H, GROUP)):
        for load in loads[n]:
            load.wait()
        for h in range(h0, h0 + GROUP):
            cols = slice(h * D, (h + 1) * D)
            prod = g_ref[:, cols].astype(F32) * o_ref[:, cols].astype(F32)
            top = prod.astype(BF16)
            rest = (prod - top.astype(F32)).astype(BF16)
            pick = jnp.where(rows == h, 1.0, 0.0).astype(BF16)
            row_dot += dot_t(pick, jnp.concatenate([top, rest], 1))
    load_l.wait()
    stat_ref[0:H, :] = l_ref[...] * LOG2E
    stat_ref[H : 2 * H, :] = row_dot
    stat_ref[2 * H :, :] = jnp.full((H, T), piece_of(message).astype(F32), F32)
    load_q.wait()


def own_half(h0, q_ref, g_ref, stat_t, low_ref, high_ref, dq_ref, low_total, high_total):
    ql = low_row(piece_of(low_ref))
    qh = pl.multiple_of(HALF - ql, HALF)
    mask = lax.broadcasted_iota(jnp.int32, (HALF, HALF), 1) <= lax.broadcasted_iota(
        jnp.int32, (HALF, HALF), 0
    )
    kl, vl = low_ref[:HALF, :], low_ref[HALF:T, :]
    kh, vh = high_ref[:HALF, :], high_ref[HALF:, :]
    heads = [slice(h * D, (h + 1) * D) for h in range(h0, h0 + GROUP)]
    q0, q1 = ([q_ref[pl.ds(rows, HALF), cols] for cols in heads] for rows in (ql, qh))
    g0, g1 = ([g_ref[pl.ds(rows, HALF), cols] for cols in heads] for rows in (ql, qh))
    scores_l, grads_l = products(q0 + q1, kl.T), products(g0 + g1, vl.T)
    scores_h, grads_h = products(q1, kh.T), products(g1, vh.T)
    p_l, d_l, p_h, d_h = [], [], [], []
    for n in range(2 * GROUP):
        rows, masked = (ql, mask) if n < GROUP else (qh, None)
        stat = stat_of(stat_t, rows, h0 + n % GROUP)
        p, d = weights_of(scores_l[n], grads_l[n], *stat, masked)
        p_l, d_l = p_l + [p], d_l + [d]
    for n in range(GROUP):
        p, d = weights_of(scores_h[n], grads_h[n], *stat_of(stat_t, qh, h0 + n), mask)
        p_h, d_h = p_h + [p], d_h + [d]
    lows = products(d_l[:GROUP], kl)
    highs = products(
        [jnp.concatenate([d_l[GROUP + n], d_h[n]], 1) for n in range(GROUP)],
        jnp.concatenate([kl, kh], 0),
    )
    for n, cols in enumerate(heads):
        dq_ref[pl.ds(ql, HALF), cols] = lows[n]
        dq_ref[pl.ds(qh, HALF), cols] = highs[n]
    g0_t, g1_t = cat([g.T for g in g0], 1), cat([g.T for g in g1], 1)
    q0_t, q1_t = cat([q.T for q in q0], 1), cat([q.T for q in q1], 1)
    dv_l, dv_h = dot(cat([g0_t, g1_t], 1), cat(p_l, 0)), dot(g1_t, cat(p_h, 0))
    dk_l, dk_h = dot(cat([q0_t, q1_t], 1), cat(d_l, 0)), dot(q1_t, cat(d_h, 0))
    for total, dk, dv in ((low_total, dk_l, dv_l), (high_total, dk_h, dv_h)):
        total[:HALF, :] += (dk * SCALE).T
        total[HALF:, :] += dv.T


def waits_long():
    return lax.axis_index("blk") < STEPS


def own_ahead_kernel(q_ref, g_ref, stat_ref, low_ref, high_ref, dq_ref, low_total, high_total, stat_t):
    low_total[...] = jnp.zeros((T, D), F32)
    high_total[...] = jnp.zeros((T, D), F32)

    @pl.when(waits_long())
    def _():
        transposed_stat(stat_ref, stat_t)
        own_half(0, q_ref, g_ref, stat_t, low_ref, high_ref, dq_ref, low_total, high_total)


def own_kernel(q_ref, g_ref, stat_ref, low_ref, high_ref, x_low, x_high, _, __, ___, dq_ref, low_total, high_total, stat_t):
    transposed_stat(stat_ref, stat_t)

    @pl.when(jnp.logical_not(waits_long()))
    def _():
        own_half(0, q_ref, g_ref, stat_t, low_ref, high_ref, dq_ref, low_total, high_total)

    own_half(GROUP, q_ref, g_ref, stat_t, low_ref, high_ref, dq_ref, low_total, high_total)

    @pl.when(is_even())
    def _():
        low_total[...] += x_low[...]
        high_total[...] += x_high[...]


class Queries:

    def __init__(self, q_ref, g_ref, stat_ref, theirs_low, stat_t):
        transposed_stat(stat_ref, stat_t)
        self.q_ref, self.g_ref, self.stat_t = q_ref, g_ref, stat_t
        first = jnp.max(stat_ref[2 * H :, :]).astype(jnp.int32)
        self.low = low_row(first)
        self.high = pl.multiple_of(HALF - self.low, HALF)
        self.lows = low_piece(first) > low_piece(piece_of(theirs_low))

    def quadrants(self, runs, keys, dq_ref, adds):
        k, v = keys[:HALF, :], keys[HALF:T, :]
        k_t, v_t = k.T, v.T
        heads = [slice(h * D, (h + 1) * D) for h in range(H)]
        q_t, g_t, ps, ds = [], [], [], []
        for rows in runs:
            qs = [self.q_ref[pl.ds(rows, HALF), cols] for cols in heads]
            gs = [self.g_ref[pl.ds(rows, HALF), cols] for cols in heads]
            scores, grads = products(qs, k_t), products(gs, v_t)
            for h in range(H):
                p, d = weights_of(scores[h], grads[h], *stat_of(self.stat_t, rows, h), None)
                ps, ds = ps + [p], ds + [d]
            q_t, g_t = q_t + [q.T for q in qs], g_t + [g.T for g in gs]
            for cols, x in zip(heads, products(ds[-H:], k)):
                if adds:
                    x += dq_ref[pl.ds(rows, HALF), cols].astype(F32)
                dq_ref[pl.ds(rows, HALF), cols] = x.astype(BF16)
        dv = dot(cat(g_t, 1), cat(ps, 0))
        dk = dot(cat(q_t, 1), cat(ds, 0))
        return (dk * SCALE).T, dv.T

    def low_keys(self, keys, dq_ref, total):
        @pl.when(self.lows)
        def _():
            dk, dv = self.quadrants((self.high, self.low), keys, dq_ref, False)
            total[:HALF, :] = dk
            total[HALF:, :] = dv

        @pl.when(jnp.logical_not(self.lows))
        def _():
            dq_ref[pl.ds(self.low, HALF), :] = jnp.zeros((HALF, H * D), BF16)
            dk, dv = self.quadrants((self.high,), keys, dq_ref, False)
            total[:HALF, :] = dk
            total[HALF:, :] = dv

    def high_keys(self, keys, dq_ref, total, adds):
        @pl.when(jnp.logical_not(self.lows))
        def _():
            dk, dv = self.quadrants((self.high,), keys, dq_ref, True)
            if adds:
                dk, dv = dk + total[:HALF, :], dv + total[HALF:, :]
            total[:HALF, :] = dk
            total[HALF:, :] = dv

        if not adds:

            @pl.when(self.lows)
            def _():
                total[...] = jnp.zeros((T, D), F32)


def is_even():
    return lax.axis_index("blk") % 2 == 0


def low_kernel(q_ref, g_ref, stat_ref, q2_ref, g2_ref, stat2_ref, own_low, own_high, theirs_low, keep, send, low_total, x_low, x_high, stat_t):
    Queries(q_ref, g_ref, stat_ref, theirs_low, stat_t).low_keys(theirs_low, keep, low_total)
    even = is_even()

    @pl.when(even)
    def _():
        queries = Queries(q2_ref, g2_ref, stat2_ref, own_low, stat_t)
        queries.low_keys(own_low, send, x_low)
        queries.high_keys(own_high, send, x_high, False)

    @pl.when(jnp.logical_not(even))
    def _():
        Queries(q2_ref, g2_ref, stat2_ref, theirs_low, stat_t).low_keys(theirs_low, send, x_low)


def high_kernel(q_ref, g_ref, stat_ref, q2_ref, g2_ref, stat2_ref, theirs_low, theirs_high, low_total, x_low, _, __, keep, send, back, high_total, stat_t):
    even = is_even()
    Queries(q_ref, g_ref, stat_ref, theirs_low, stat_t).high_keys(
        theirs_high, keep, high_total, False
    )

    @pl.when(even)
    def _():
        back[:T, :] = low_total[...].astype(BF16)

    @pl.when(jnp.logical_not(even))
    def _():
        back[:T, :] = (low_total[...] + x_low[...]).astype(BF16)
        others = Queries(q2_ref, g2_ref, stat2_ref, theirs_low, stat_t)
        others.high_keys(theirs_high, send, high_total, True)

    back[T:, :] = high_total[...].astype(BF16)


def query_kernel(dq_ref, keep_ref, got_ref, out_hbm, out_ref, sems):
    copies = []
    for n in range(4):
        rows = pl.ds(n * T // 4, T // 4)
        total = dq_ref[rows, :] + keep_ref[rows, :].astype(F32) + got_ref[rows, :].astype(F32)
        out_ref[rows, :] = (total * SCALE).astype(BF16)
        copies.append(pltpu.make_async_copy(out_ref.at[rows, :], out_hbm.at[rows, :], sems.at[n]))
        copies[n].start()
    for copy in copies:
        copy.wait()


def key_kernel(own_low, low_total, high_total, got_ref, dk_ref, dv_ref):
    ql = low_row(piece_of(own_low))
    qh = pl.multiple_of(HALF - ql, HALF)
    for total, rows, at in ((low_total, ql, 0), (high_total, qh, T)):
        for out, n in ((dk_ref, 0), (dv_ref, HALF)):
            got = got_ref[at + n : at + n + HALF, :].astype(F32)
            out[pl.ds(rows, HALF), :] = (total[n : n + HALF, :] + got).astype(BF16)


def vmem():
    return pl.BlockSpec(memory_space=pltpu.VMEM)


def cost(quadrants, size):
    return pl.CostEstimate(
        flops=int(quadrants * H * 10 * HALF * HALF * D),
        bytes_accessed=size,
        transcendentals=int(quadrants * H * HALF * HALF),
    )


def hbm():
    return pl.BlockSpec(memory_space=pltpu.HBM)


def pack(k, v, positions):
    return pl.pallas_call(
        pack_kernel,
        in_specs=[hbm()] * 3,
        out_specs=vmem(),
        out_shape=jax.ShapeDtypeStruct((2 * T + IDS, D), BF16),
        scratch_shapes=[pltpu.SMEM(positions.shape, jnp.int32), pltpu.SemaphoreType.DMA((3,))],
        name="pack",
    )(k, v, positions)


def hbm():
    return pl.BlockSpec(memory_space=pltpu.HBM)


def in_vmem(value):
    return pltpu.with_memory_space_constraint(value, pltpu.VMEM)


def array(shape, dtype):
    return jax.ShapeDtypeStruct(shape, dtype)


def call(kernel, name, ins, outs, scratch=(), quadrants=0, from_hbm=0, to_hbm=0, aliases=None):
    size = sum(x.size * x.dtype.itemsize for x in list(ins) + list(outs))
    return pl.pallas_call(
        kernel,
        in_specs=[hbm()] * from_hbm + [vmem()] * (len(ins) - from_hbm),
        out_specs=[hbm()] * to_hbm + [vmem()] * (len(outs) - to_hbm),
        out_shape=list(outs),
        scratch_shapes=list(scratch),
        input_output_aliases=aliases or {},
        compiler_params=pltpu.CompilerParams(vmem_limit_bytes=24 << 20),
        cost_estimate=cost(quadrants, size),
        name=name,
    )(*ins)


def passed_along(value, steps):
    count = lax.axis_size("blk")
    pairs = [(source, (source + steps) % count) for source in range(count)]
    return lax.ppermute(value, "blk", pairs)


def swapped(value):
    count = lax.axis_size("blk")
    return lax.ppermute(value, "blk", [(source, source ^ 1) for source in range(count)])


def on_device(q_in, k, v, o, g_in, log_total, positions):
    q_in, k, v, o, g_in, log_total, positions = (
        pltpu.with_memory_space_constraint(x, pltpu.HBM)
        for x in (q_in, k, v, o, g_in, log_total, positions)
    )
    rows = array((T, H * D), BF16)
    stat_t = pltpu.VMEM((T, 3 * H), F32)
    terms, half_terms = array((2 * T, D), F32), array((T, D), F32)
    low, high = call(
        pack_kernel,
        "pack",
        (k, v, positions),
        (array((T + IDS, D), BF16), array((T, D), BF16)),
        (
            pltpu.SMEM(positions.shape, jnp.int32),
            pltpu.VMEM((T, D), BF16),
            pltpu.VMEM((T, D), BF16),
            pltpu.SemaphoreType.DMA((3,)),
        ),
        from_hbm=3,
    )
    theirs_low = in_vmem(passed_along(low, 2))
    low, q_swap, g_swap = lax.optimization_barrier((low, q_in, g_in))
    q2, g2 = in_vmem(swapped(q_swap)), in_vmem(swapped(g_swap))
    q, g, stat = call(
        stat_kernel,
        "stat",
        (q_in, g_in, o, log_total, low),
        (rows, rows, array((3 * H, T), F32)),
        (pltpu.VMEM((T, H * D), BF16), pltpu.VMEM((H, T), F32), pltpu.SemaphoreType.DMA((2, 3))),
        quadrants=30,
        from_hbm=4,
    )
    high, stat = lax.optimization_barrier((high, stat))
    theirs_high = in_vmem(passed_along(high, 2))
    stat2 = in_vmem(swapped(stat))
    own_out = (array((T, H * D), F32), half_terms, half_terms)
    dq, own_low, own_high = call(
        own_ahead_kernel,
        "own_ahead",
        (q, g, stat, low, high),
        own_out,
        (stat_t,),
    )
    theirs_low, dq = lax.optimization_barrier((theirs_low, dq))
    keep, send, low_total, x_low, x_high = call(
        low_kernel,
        "low_keys",
        (q, g, stat, q2, g2, stat2, low, high, theirs_low),
        (rows, rows, half_terms, half_terms, half_terms),
        (stat_t,),
        quadrants=3.5,
    )
    theirs_high, send = lax.optimization_barrier((theirs_high, send))
    keep, send, message_back = call(
        high_kernel,
        "high_keys",
        (q, g, stat, q2, g2, stat2, theirs_low, theirs_high, low_total, x_low, keep, send),
        (rows, rows, array((2 * T, D), BF16)),
        (pltpu.VMEM((T, D), F32), stat_t),
        quadrants=0.5,
        aliases={10: 0, 11: 1},
    )
    back = passed_along(message_back, -2)
    got = in_vmem(swapped(send))
    dq, own_low, own_high = call(
        own_kernel,
        "own",
        (q, g, stat, low, high, x_low, x_high, dq, own_low, own_high),
        own_out,
        (stat_t,),
        quadrants=60,
        aliases={7: 0, 8: 1, 9: 2},
    )
    (dq,) = call(
        query_kernel,
        "query_sum",
        (dq, keep, got),
        (rows,),
        (pltpu.VMEM((T, H * D), BF16), pltpu.SemaphoreType.DMA((4,))),
        to_hbm=1,
    )
    back, dq = lax.optimization_barrier((back, dq))
    dk, dv = call(
        key_kernel, "key_sum", (low, own_low, own_high, back), (array((T, D), BF16),) * 2
    )
    return dq, dk, dv


def solution(mesh):
    in_specs = (
        P("blk", "tp"),
        P("blk", "tp"),
        P("blk", "tp"),
        P("blk", "tp"),
        P("blk", "tp"),
        P("tp", "blk"),
        P(("blk", "tp")),
    )
    out_specs = (P("blk", "tp"), P("blk", "tp"), P("blk", "tp"))
    return jax.shard_map(
        on_device, mesh=mesh, in_specs=in_specs, out_specs=out_specs, check_vma=False
    )
```

```python
import functools
import math

import jax
import jax.numpy as jnp
from jax import lax
from jax.experimental import pallas as pl
from jax.experimental.pallas import tpu as pltpu
from jax.sharding import PartitionSpec as P

D = 128
H = 8
T = 512
STEPS = 2
HALF = T // 2
PIECES = 64
IDS = 16
GROUP = 4
SCALE = 1.0 / math.sqrt(D)
LOG2E = math.log2(math.e)
SCORE_SCALE = SCALE * LOG2E
F32 = jnp.float32
BF16 = jnp.bfloat16


def dot(a, b):
    return lax.dot_general(a, b, (((1,), (0,)), ((), ())), preferred_element_type=F32)


def dot_t(a, b):
    return lax.dot_general(a, b, (((1,), (1,)), ((), ())), preferred_element_type=F32)


def cat(parts, axis):
    return parts[0] if len(parts) == 1 else jnp.concatenate(parts, axis)


def products(parts, matrix):
    whole = dot(cat(parts, 0), matrix)
    return [whole[n * HALF : (n + 1) * HALF, :] for n in range(len(parts))]


def weights_of(scores, grads, log_total, row_dot, mask):
    p = jnp.exp2(scores * SCORE_SCALE - log_total)
    if mask is not None:
        p = jnp.where(mask, p, 0.0)
    ds = p * (grads - row_dot)
    return p.astype(BF16), ds.astype(BF16)


def piece_of(message):
    return jnp.max(message[T:, :].astype(F32)).astype(jnp.int32)


def low_row(first):
    return pl.multiple_of(jnp.where(first < PIECES // 2, 0, HALF), HALF)


def low_piece(first):
    return jnp.minimum(first, PIECES - 1 - first)


def pack_kernel(k_hbm, v_hbm, pos_hbm, low, high, pos, k_ref, v_ref, sems):
    copies = [
        pltpu.make_async_copy(source, target, sems.at[i])
        for i, (source, target) in enumerate(((pos_hbm, pos), (k_hbm, k_ref), (v_hbm, v_ref)))
    ]
    for copy in copies:
        copy.start()
    copies[0].wait()
    piece = pos[0] // HALF
    in_first = lax.axis_index("tp") < lax.axis_size("tp") // 2
    first = jnp.where(in_first, piece, PIECES - 1 - piece)
    low[T:, :] = jnp.full((IDS, D), first.astype(F32), F32).astype(BF16)
    ql = low_row(first)
    qh = pl.multiple_of(HALF - ql, HALF)
    for copy, source, at in ((copies[1], k_ref, 0), (copies[2], v_ref, HALF)):
        copy.wait()
        low[at : at + HALF, :] = source[pl.ds(ql, HALF), :]
        high[at : at + HALF, :] = source[pl.ds(qh, HALF), :]


def transposed_stat(stat_ref, stat_t):
    stat_t[...] = stat_ref[...].T


def stat_of(stat_t, rows, h):
    return stat_t[pl.ds(rows, HALF), h : h + 1], stat_t[pl.ds(rows, HALF), H + h : H + h + 1]


def stat_kernel(q_hbm, g_hbm, o_hbm, l_hbm, message, q_ref, g_ref, stat_ref, o_ref, l_ref, sems):
    load_l = pltpu.make_async_copy(l_hbm, l_ref, sems.at[0, 2])
    load_q = pltpu.make_async_copy(q_hbm, q_ref, sems.at[1, 2])
    loads = []
    for n, h0 in enumerate(range(0, H, GROUP)):
        cols = pl.ds(h0 * D, GROUP * D)
        loads.append(
            [
                pltpu.make_async_copy(source.at[:, cols], target.at[:, cols], sems.at[n, i])
                for i, (source, target) in enumerate(((g_hbm, g_ref), (o_hbm, o_ref)))
            ]
        )
        for load in loads[n]:
            load.start()
    load_l.start()
    load_q.start()
    rows = lax.broadcasted_iota(jnp.int32, (H, 2 * D), 0)
    row_dot = jnp.zeros((H, T), F32)
    for n, h0 in enumerate(range(0, H, GROUP)):
        for load in loads[n]:
            load.wait()
        for h in range(h0, h0 + GROUP):
            cols = slice(h * D, (h + 1) * D)
            prod = g_ref[:, cols].astype(F32) * o_ref[:, cols].astype(F32)
            top = prod.astype(BF16)
            rest = (prod - top.astype(F32)).astype(BF16)
            pick = jnp.where(rows == h, 1.0, 0.0).astype(BF16)
            row_dot += dot_t(pick, jnp.concatenate([top, rest], 1))
    load_l.wait()
    stat_ref[0:H, :] = l_ref[...] * LOG2E
    stat_ref[H : 2 * H, :] = row_dot
    stat_ref[2 * H :, :] = jnp.full((H, T), piece_of(message).astype(F32), F32)
    load_q.wait()


def own_half(h0, q_ref, g_ref, stat_t, low_ref, high_ref, dq_ref, low_total, high_total):
    ql = low_row(piece_of(low_ref))
    qh = pl.multiple_of(HALF - ql, HALF)
    mask = lax.broadcasted_iota(jnp.int32, (HALF, HALF), 1) <= lax.broadcasted_iota(
        jnp.int32, (HALF, HALF), 0
    )
    kl, vl = low_ref[:HALF, :], low_ref[HALF:T, :]
    kh, vh = high_ref[:HALF, :], high_ref[HALF:, :]
    heads = [slice(h * D, (h + 1) * D) for h in range(h0, h0 + GROUP)]
    q0, q1 = ([q_ref[pl.ds(rows, HALF), cols] for cols in heads] for rows in (ql, qh))
    g0, g1 = ([g_ref[pl.ds(rows, HALF), cols] for cols in heads] for rows in (ql, qh))
    scores_l, grads_l = products(q0 + q1, kl.T), products(g0 + g1, vl.T)
    scores_h, grads_h = products(q1, kh.T), products(g1, vh.T)
    p_l, d_l, p_h, d_h = [], [], [], []
    for n in range(2 * GROUP):
        rows, masked = (ql, mask) if n < GROUP else (qh, None)
        stat = stat_of(stat_t, rows, h0 + n % GROUP)
        p, d = weights_of(scores_l[n], grads_l[n], *stat, masked)
        p_l, d_l = p_l + [p], d_l + [d]
    for n in range(GROUP):
        p, d = weights_of(scores_h[n], grads_h[n], *stat_of(stat_t, qh, h0 + n), mask)
        p_h, d_h = p_h + [p], d_h + [d]
    lows = products(d_l[:GROUP], kl)
    highs = products(
        [jnp.concatenate([d_l[GROUP + n], d_h[n]], 1) for n in range(GROUP)],
        jnp.concatenate([kl, kh], 0),
    )
    for n, cols in enumerate(heads):
        dq_ref[pl.ds(ql, HALF), cols] = lows[n]
        dq_ref[pl.ds(qh, HALF), cols] = highs[n]
    g0_t, g1_t = cat([g.T for g in g0], 1), cat([g.T for g in g1], 1)
    q0_t, q1_t = cat([q.T for q in q0], 1), cat([q.T for q in q1], 1)
    dv_l, dv_h = dot(cat([g0_t, g1_t], 1), cat(p_l, 0)), dot(g1_t, cat(p_h, 0))
    dk_l, dk_h = dot(cat([q0_t, q1_t], 1), cat(d_l, 0)), dot(q1_t, cat(d_h, 0))
    for total, dk, dv in ((low_total, dk_l, dv_l), (high_total, dk_h, dv_h)):
        total[:HALF, :] += (dk * SCALE).T
        total[HALF:, :] += dv.T


def waits_long():
    return lax.axis_index("blk") < STEPS


def own_ahead_kernel(q_ref, g_ref, stat_ref, low_ref, high_ref, dq_ref, low_total, high_total, stat_t):
    low_total[...] = jnp.zeros((T, D), F32)
    high_total[...] = jnp.zeros((T, D), F32)

    @pl.when(waits_long())
    def _():
        transposed_stat(stat_ref, stat_t)
        own_half(0, q_ref, g_ref, stat_t, low_ref, high_ref, dq_ref, low_total, high_total)


def own_kernel(q_ref, g_ref, stat_ref, low_ref, high_ref, x_low, x_high, _, __, ___, dq_ref, low_total, high_total, stat_t):
    transposed_stat(stat_ref, stat_t)

    @pl.when(jnp.logical_not(waits_long()))
    def _():
        own_half(0, q_ref, g_ref, stat_t, low_ref, high_ref, dq_ref, low_total, high_total)

    own_half(GROUP, q_ref, g_ref, stat_t, low_ref, high_ref, dq_ref, low_total, high_total)

    @pl.when(is_even())
    def _():
        for total, more in ((low_total, x_low), (high_total, x_high)):
            total[:HALF, :] += more[:D, :].T
            total[HALF:, :] += more[D:, :].T


class Queries:

    def __init__(self, q_ref, g_ref, stat_ref, theirs_low, stat_t):
        transposed_stat(stat_ref, stat_t)
        self.q_ref, self.g_ref, self.stat_t = q_ref, g_ref, stat_t
        first = jnp.max(stat_ref[2 * H :, :]).astype(jnp.int32)
        self.low = low_row(first)
        self.high = pl.multiple_of(HALF - self.low, HALF)
        self.lows = low_piece(first) > low_piece(piece_of(theirs_low))

    def quadrants(self, runs, keys, dq_ref, adds):
        k, v = keys[:HALF, :], keys[HALF:T, :]
        k_t, v_t = k.T, v.T
        heads = [slice(h * D, (h + 1) * D) for h in range(H)]
        q_t, g_t, ps, ds = [], [], [], []
        for rows in runs:
            qs = [self.q_ref[pl.ds(rows, HALF), cols] for cols in heads]
            gs = [self.g_ref[pl.ds(rows, HALF), cols] for cols in heads]
            scores, grads = products(qs, k_t), products(gs, v_t)
            for h in range(H):
                p, d = weights_of(scores[h], grads[h], *stat_of(self.stat_t, rows, h), None)
                ps, ds = ps + [p], ds + [d]
            q_t, g_t = q_t + [q.T for q in qs], g_t + [g.T for g in gs]
            for cols, x in zip(heads, products(ds[-H:], k)):
                if adds:
                    x += dq_ref[pl.ds(rows, HALF), cols].astype(F32)
                dq_ref[pl.ds(rows, HALF), cols] = x.astype(BF16)
        dv = dot(cat(g_t, 1), cat(ps, 0))
        dk = dot(cat(q_t, 1), cat(ds, 0))
        return dk * SCALE, dv

    def low_keys(self, keys, dq_ref, total):
        @pl.when(self.lows)
        def _():
            dk, dv = self.quadrants((self.high, self.low), keys, dq_ref, False)
            total[:D, :] = dk
            total[D:, :] = dv

        @pl.when(jnp.logical_not(self.lows))
        def _():
            dq_ref[pl.ds(self.low, HALF), :] = jnp.zeros((HALF, H * D), BF16)
            dk, dv = self.quadrants((self.high,), keys, dq_ref, False)
            total[:D, :] = dk
            total[D:, :] = dv

    def high_keys(self, keys, dq_ref, total, adds):
        @pl.when(jnp.logical_not(self.lows))
        def _():
            dk, dv = self.quadrants((self.high,), keys, dq_ref, True)
            if adds:
                dk, dv = dk + total[:D, :], dv + total[D:, :]
            total[:D, :] = dk
            total[D:, :] = dv

        if not adds:

            @pl.when(self.lows)
            def _():
                total[...] = jnp.zeros((2 * D, HALF), F32)


def is_even():
    return lax.axis_index("blk") % 2 == 0


def low_kernel(q_ref, g_ref, stat_ref, q2_ref, g2_ref, stat2_ref, own_low, own_high, theirs_low, keep, send, low_total, x_low, x_high, stat_t):
    Queries(q_ref, g_ref, stat_ref, theirs_low, stat_t).low_keys(theirs_low, keep, low_total)
    even = is_even()

    @pl.when(even)
    def _():
        queries = Queries(q2_ref, g2_ref, stat2_ref, own_low, stat_t)
        queries.low_keys(own_low, send, x_low)
        queries.high_keys(own_high, send, x_high, False)

    @pl.when(jnp.logical_not(even))
    def _():
        Queries(q2_ref, g2_ref, stat2_ref, theirs_low, stat_t).low_keys(theirs_low, send, x_low)


def write_back(back, at, total):
    back[at : at + HALF, :] = total[:D, :].T.astype(BF16)
    back[at + HALF : at + T, :] = total[D:, :].T.astype(BF16)


def high_kernel(q_ref, g_ref, stat_ref, q2_ref, g2_ref, stat2_ref, theirs_low, theirs_high, low_total, x_low, _, __, keep, send, back, high_total, stat_t):
    even = is_even()
    Queries(q_ref, g_ref, stat_ref, theirs_low, stat_t).high_keys(
        theirs_high, keep, high_total, False
    )

    @pl.when(even)
    def _():
        write_back(back, 0, low_total[...])

    @pl.when(jnp.logical_not(even))
    def _():
        write_back(back, 0, low_total[...] + x_low[...])
        others = Queries(q2_ref, g2_ref, stat2_ref, theirs_low, stat_t)
        others.high_keys(theirs_high, send, high_total, True)

    write_back(back, T, high_total[...])


def query_kernel(dq_ref, keep_ref, got_ref, out_hbm, out_ref, sems):
    copies = []
    for n in range(4):
        rows = pl.ds(n * T // 4, T // 4)
        total = dq_ref[rows, :] + keep_ref[rows, :].astype(F32) + got_ref[rows, :].astype(F32)
        out_ref[rows, :] = (total * SCALE).astype(BF16)
        copies.append(pltpu.make_async_copy(out_ref.at[rows, :], out_hbm.at[rows, :], sems.at[n]))
        copies[n].start()
    for copy in copies:
        copy.wait()


def key_kernel(own_low, low_total, high_total, got_ref, dk_ref, dv_ref):
    ql = low_row(piece_of(own_low))
    qh = pl.multiple_of(HALF - ql, HALF)
    for total, rows, at in ((low_total, ql, 0), (high_total, qh, T)):
        for out, n in ((dk_ref, 0), (dv_ref, HALF)):
            got = got_ref[at + n : at + n + HALF, :].astype(F32)
            out[pl.ds(rows, HALF), :] = (total[n : n + HALF, :] + got).astype(BF16)


def vmem():
    return pl.BlockSpec(memory_space=pltpu.VMEM)


def cost(quadrants, size):
    return pl.CostEstimate(
        flops=int(quadrants * H * 10 * HALF * HALF * D),
        bytes_accessed=size,
        transcendentals=int(quadrants * H * HALF * HALF),
    )


def hbm():
    return pl.BlockSpec(memory_space=pltpu.HBM)


def pack(k, v, positions):
    return pl.pallas_call(
        pack_kernel,
        in_specs=[hbm()] * 3,
        out_specs=vmem(),
        out_shape=jax.ShapeDtypeStruct((2 * T + IDS, D), BF16),
        scratch_shapes=[pltpu.SMEM(positions.shape, jnp.int32), pltpu.SemaphoreType.DMA((3,))],
        name="pack",
    )(k, v, positions)


def hbm():
    return pl.BlockSpec(memory_space=pltpu.HBM)


def in_vmem(value):
    return pltpu.with_memory_space_constraint(value, pltpu.VMEM)


def array(shape, dtype):
    return jax.ShapeDtypeStruct(shape, dtype)


def call(kernel, name, ins, outs, scratch=(), quadrants=0, from_hbm=0, to_hbm=0, aliases=None):
    size = sum(x.size * x.dtype.itemsize for x in list(ins) + list(outs))
    return pl.pallas_call(
        kernel,
        in_specs=[hbm()] * from_hbm + [vmem()] * (len(ins) - from_hbm),
        out_specs=[hbm()] * to_hbm + [vmem()] * (len(outs) - to_hbm),
        out_shape=list(outs),
        scratch_shapes=list(scratch),
        input_output_aliases=aliases or {},
        compiler_params=pltpu.CompilerParams(vmem_limit_bytes=24 << 20),
        cost_estimate=cost(quadrants, size),
        name=name,
    )(*ins)


def passed_along(value, steps):
    count = lax.axis_size("blk")
    pairs = [(source, (source + steps) % count) for source in range(count)]
    return lax.ppermute(value, "blk", pairs)


def swapped(value):
    count = lax.axis_size("blk")
    return lax.ppermute(value, "blk", [(source, source ^ 1) for source in range(count)])


def on_device(q_in, k, v, o, g_in, log_total, positions):
    q_in, k, v, o, g_in, log_total, positions = (
        pltpu.with_memory_space_constraint(x, pltpu.HBM)
        for x in (q_in, k, v, o, g_in, log_total, positions)
    )
    rows = array((T, H * D), BF16)
    stat_t = pltpu.VMEM((T, 3 * H), F32)
    terms, half_terms = array((2 * T, D), F32), array((T, D), F32)
    low, high = call(
        pack_kernel,
        "pack",
        (k, v, positions),
        (array((T + IDS, D), BF16), array((T, D), BF16)),
        (
            pltpu.SMEM(positions.shape, jnp.int32),
            pltpu.VMEM((T, D), BF16),
            pltpu.VMEM((T, D), BF16),
            pltpu.SemaphoreType.DMA((3,)),
        ),
        from_hbm=3,
    )
    theirs_low = in_vmem(passed_along(low, 2))
    low, q_swap, g_swap = lax.optimization_barrier((low, q_in, g_in))
    q2, g2 = in_vmem(swapped(q_swap)), in_vmem(swapped(g_swap))
    q, g, stat = call(
        stat_kernel,
        "stat",
        (q_in, g_in, o, log_total, low),
        (rows, rows, array((3 * H, T), F32)),
        (pltpu.VMEM((T, H * D), BF16), pltpu.VMEM((H, T), F32), pltpu.SemaphoreType.DMA((2, 3))),
        quadrants=30,
        from_hbm=4,
    )
    high, stat = lax.optimization_barrier((high, stat))
    theirs_high = in_vmem(passed_along(high, 2))
    stat2 = in_vmem(swapped(stat))
    own_out = (array((T, H * D), F32), half_terms, half_terms)
    dq, own_low, own_high = call(
        own_ahead_kernel,
        "own_ahead",
        (q, g, stat, low, high),
        own_out,
        (stat_t,),
    )
    theirs_low, dq = lax.optimization_barrier((theirs_low, dq))
    keep, send, low_total, x_low, x_high = call(
        low_kernel,
        "low_keys",
        (q, g, stat, q2, g2, stat2, low, high, theirs_low),
        (rows, rows) + (array((2 * D, HALF), F32),) * 3,
        (stat_t,),
        quadrants=3.5,
    )
    theirs_high, send = lax.optimization_barrier((theirs_high, send))
    keep, send, message_back = call(
        high_kernel,
        "high_keys",
        (q, g, stat, q2, g2, stat2, theirs_low, theirs_high, low_total, x_low, keep, send),
        (rows, rows, array((2 * T, D), BF16)),
        (pltpu.VMEM((2 * D, HALF), F32), stat_t),
        quadrants=0.5,
        aliases={10: 0, 11: 1},
    )
    back = passed_along(message_back, -2)
    got = in_vmem(swapped(send))
    dq, own_low, own_high = call(
        own_kernel,
        "own",
        (q, g, stat, low, high, x_low, x_high, dq, own_low, own_high),
        own_out,
        (stat_t,),
        quadrants=60,
        aliases={7: 0, 8: 1, 9: 2},
    )
    (dq,) = call(
        query_kernel,
        "query_sum",
        (dq, keep, got),
        (rows,),
        (pltpu.VMEM((T, H * D), BF16), pltpu.SemaphoreType.DMA((4,))),
        to_hbm=1,
    )
    back, dq = lax.optimization_barrier((back, dq))
    dk, dv = call(
        key_kernel, "key_sum", (low, own_low, own_high, back), (array((T, D), BF16),) * 2
    )
    return dq, dk, dv


def solution(mesh):
    in_specs = (
        P("blk", "tp"),
        P("blk", "tp"),
        P("blk", "tp"),
        P("blk", "tp"),
        P("blk", "tp"),
        P("tp", "blk"),
        P(("blk", "tp")),
    )
    out_specs = (P("blk", "tp"), P("blk", "tp"), P("blk", "tp"))
    return jax.shard_map(
        on_device, mesh=mesh, in_specs=in_specs, out_specs=out_specs, check_vma=False
    )
```

```python
import functools
import math

import jax
import jax.numpy as jnp
from jax import lax
from jax.experimental import pallas as pl
from jax.experimental.pallas import tpu as pltpu
from jax.sharding import PartitionSpec as P

D = 128
H = 8
T = 512
STEPS = 2
HALF = T // 2
PIECES = 64
IDS = 16
GROUP = 4
SCALE = 1.0 / math.sqrt(D)
LOG2E = math.log2(math.e)
SCORE_SCALE = SCALE * LOG2E
F32 = jnp.float32
BF16 = jnp.bfloat16


def dot(a, b):
    return lax.dot_general(a, b, (((1,), (0,)), ((), ())), preferred_element_type=F32)


def dot_t(a, b):
    return lax.dot_general(a, b, (((1,), (1,)), ((), ())), preferred_element_type=F32)


def cat(parts, axis):
    return parts[0] if len(parts) == 1 else jnp.concatenate(parts, axis)


def products(parts, matrix):
    whole = dot(cat(parts, 0), matrix)
    return [whole[n * HALF : (n + 1) * HALF, :] for n in range(len(parts))]


def weights_of(scores, grads, log_total, row_dot, mask):
    p = jnp.exp2(scores * SCORE_SCALE - log_total)
    if mask is not None:
        p = jnp.where(mask, p, 0.0)
    ds = p * (grads - row_dot)
    return p.astype(BF16), ds.astype(BF16)


def piece_of(message):
    return jnp.max(message[T:, :].astype(F32)).astype(jnp.int32)


def low_row(first):
    return pl.multiple_of(jnp.where(first < PIECES // 2, 0, HALF), HALF)


def low_piece(first):
    return jnp.minimum(first, PIECES - 1 - first)


def pack_kernel(k_hbm, v_hbm, pos_hbm, low, high, pos, k_ref, v_ref, sems):
    copies = [
        pltpu.make_async_copy(source, target, sems.at[i])
        for i, (source, target) in enumerate(((pos_hbm, pos), (k_hbm, k_ref), (v_hbm, v_ref)))
    ]
    for copy in copies:
        copy.start()
    copies[0].wait()
    piece = pos[0] // HALF
    in_first = lax.axis_index("tp") < lax.axis_size("tp") // 2
    first = jnp.where(in_first, piece, PIECES - 1 - piece)
    low[T:, :] = jnp.full((IDS, D), first.astype(F32), F32).astype(BF16)
    ql = low_row(first)
    qh = pl.multiple_of(HALF - ql, HALF)
    for copy, source, at in ((copies[1], k_ref, 0), (copies[2], v_ref, HALF)):
        copy.wait()
        low[at : at + HALF, :] = source[pl.ds(ql, HALF), :]
        high[at : at + HALF, :] = source[pl.ds(qh, HALF), :]


def transposed_stat(stat_ref, stat_t):
    stat_t[...] = stat_ref[...].T


def stat_of(stat_t, rows, h):
    return stat_t[pl.ds(rows, HALF), h : h + 1], stat_t[pl.ds(rows, HALF), H + h : H + h + 1]


def stat_kernel(q_hbm, g_hbm, o_hbm, l_hbm, message, q_ref, g_ref, stat_ref, o_ref, l_ref, sems):
    load_l = pltpu.make_async_copy(l_hbm, l_ref, sems.at[0, 2])
    load_q = pltpu.make_async_copy(q_hbm, q_ref, sems.at[1, 2])
    loads = []
    for n, h0 in enumerate(range(0, H, GROUP)):
        cols = pl.ds(h0 * D, GROUP * D)
        loads.append(
            [
                pltpu.make_async_copy(source.at[:, cols], target.at[:, cols], sems.at[n, i])
                for i, (source, target) in enumerate(((g_hbm, g_ref), (o_hbm, o_ref)))
            ]
        )
        for load in loads[n]:
            load.start()
    load_l.start()
    load_q.start()
    rows = lax.broadcasted_iota(jnp.int32, (H, 2 * D), 0)
    row_dot = jnp.zeros((H, T), F32)
    for n, h0 in enumerate(range(0, H, GROUP)):
        for load in loads[n]:
            load.wait()
        for h in range(h0, h0 + GROUP):
            cols = slice(h * D, (h + 1) * D)
            prod = g_ref[:, cols].astype(F32) * o_ref[:, cols].astype(F32)
            top = prod.astype(BF16)
            rest = (prod - top.astype(F32)).astype(BF16)
            pick = jnp.where(rows == h, 1.0, 0.0).astype(BF16)
            row_dot += dot_t(pick, jnp.concatenate([top, rest], 1))
    load_l.wait()
    stat_ref[0:H, :] = l_ref[...] * LOG2E
    stat_ref[H : 2 * H, :] = row_dot
    stat_ref[2 * H :, :] = jnp.full((H, T), piece_of(message).astype(F32), F32)
    load_q.wait()


def own_half(h0, q_ref, g_ref, stat_t, low_ref, high_ref, dq_ref, low_total, high_total):
    ql = low_row(piece_of(low_ref))
    qh = pl.multiple_of(HALF - ql, HALF)
    mask = lax.broadcasted_iota(jnp.int32, (HALF, HALF), 1) <= lax.broadcasted_iota(
        jnp.int32, (HALF, HALF), 0
    )
    kl, vl = low_ref[:HALF, :], low_ref[HALF:T, :]
    kh, vh = high_ref[:HALF, :], high_ref[HALF:, :]
    heads = [slice(h * D, (h + 1) * D) for h in range(h0, h0 + GROUP)]
    q0, q1 = ([q_ref[pl.ds(rows, HALF), cols] for cols in heads] for rows in (ql, qh))
    g0, g1 = ([g_ref[pl.ds(rows, HALF), cols] for cols in heads] for rows in (ql, qh))
    scores_l, grads_l = products(q0 + q1, kl.T), products(g0 + g1, vl.T)
    scores_h, grads_h = products(q1, kh.T), products(g1, vh.T)
    p_l, d_l, p_h, d_h = [], [], [], []
    for n in range(2 * GROUP):
        rows, masked = (ql, mask) if n < GROUP else (qh, None)
        stat = stat_of(stat_t, rows, h0 + n % GROUP)
        p, d = weights_of(scores_l[n], grads_l[n], *stat, masked)
        p_l, d_l = p_l + [p], d_l + [d]
    for n in range(GROUP):
        p, d = weights_of(scores_h[n], grads_h[n], *stat_of(stat_t, qh, h0 + n), mask)
        p_h, d_h = p_h + [p], d_h + [d]
    lows = products(d_l[:GROUP], kl)
    highs = products(
        [jnp.concatenate([d_l[GROUP + n], d_h[n]], 1) for n in range(GROUP)],
        jnp.concatenate([kl, kh], 0),
    )
    for n, cols in enumerate(heads):
        dq_ref[pl.ds(ql, HALF), cols] = lows[n]
        dq_ref[pl.ds(qh, HALF), cols] = highs[n]
    g0_t, g1_t = cat([g.T for g in g0], 1), cat([g.T for g in g1], 1)
    q0_t, q1_t = cat([q.T for q in q0], 1), cat([q.T for q in q1], 1)
    dv_l, dv_h = dot(cat([g0_t, g1_t], 1), cat(p_l, 0)), dot(g1_t, cat(p_h, 0))
    dk_l, dk_h = dot(cat([q0_t, q1_t], 1), cat(d_l, 0)), dot(q1_t, cat(d_h, 0))
    for total, dk, dv in ((low_total, dk_l, dv_l), (high_total, dk_h, dv_h)):
        total[:HALF, :] += (dk * SCALE).T
        total[HALF:, :] += dv.T


def waits_long():
    return lax.axis_index("blk") < STEPS


def own_ahead_kernel(q_ref, g_ref, stat_ref, low_ref, high_ref, dq_ref, low_total, high_total, stat_t):
    low_total[...] = jnp.zeros((T, D), F32)
    high_total[...] = jnp.zeros((T, D), F32)

    @pl.when(waits_long())
    def _():
        transposed_stat(stat_ref, stat_t)
        own_half(0, q_ref, g_ref, stat_t, low_ref, high_ref, dq_ref, low_total, high_total)


def own_kernel(q_ref, g_ref, stat_ref, low_ref, high_ref, x_low, x_high, _, __, ___, dq_ref, low_total, high_total, stat_t):
    transposed_stat(stat_ref, stat_t)

    @pl.when(jnp.logical_not(waits_long()))
    def _():
        own_half(0, q_ref, g_ref, stat_t, low_ref, high_ref, dq_ref, low_total, high_total)

    own_half(GROUP, q_ref, g_ref, stat_t, low_ref, high_ref, dq_ref, low_total, high_total)

    @pl.when(is_even())
    def _():
        for total, more in ((low_total, x_low), (high_total, x_high)):
            total[:HALF, :] += more[:D, :].T
            total[HALF:, :] += more[D:, :].T


class Queries:

    def __init__(self, q_ref, g_ref, stat_ref, theirs_low, stat_t):
        transposed_stat(stat_ref, stat_t)
        self.q_ref, self.g_ref, self.stat_t = q_ref, g_ref, stat_t
        first = jnp.max(stat_ref[2 * H :, :]).astype(jnp.int32)
        self.low = low_row(first)
        self.high = pl.multiple_of(HALF - self.low, HALF)
        self.lows = low_piece(first) > low_piece(piece_of(theirs_low))

    def quadrants(self, runs, keys, dq_ref, adds):
        k, v = keys[:HALF, :], keys[HALF:T, :]
        k_t, v_t = k.T, v.T
        heads = [slice(h * D, (h + 1) * D) for h in range(H)]
        q_t, g_t, ps, ds = [], [], [], []
        for rows in runs:
            qs = [self.q_ref[pl.ds(rows, HALF), cols] for cols in heads]
            gs = [self.g_ref[pl.ds(rows, HALF), cols] for cols in heads]
            scores, grads = products(qs, k_t), products(gs, v_t)
            for h in range(H):
                p, d = weights_of(scores[h], grads[h], *stat_of(self.stat_t, rows, h), None)
                ps, ds = ps + [p], ds + [d]
            q_t, g_t = q_t + [q.T for q in qs], g_t + [g.T for g in gs]
            for cols, x in zip(heads, products(ds[-H:], k)):
                if adds:
                    x += dq_ref[pl.ds(rows, HALF), cols].astype(F32)
                dq_ref[pl.ds(rows, HALF), cols] = x.astype(BF16)
        dv = dot(cat(g_t, 1), cat(ps, 0))
        dk = dot(cat(q_t, 1), cat(ds, 0))
        return dk * SCALE, dv

    def low_keys(self, keys, dq_ref, total):
        @pl.when(self.lows)
        def _():
            dk, dv = self.quadrants((self.high, self.low), keys, dq_ref, False)
            total[:D, :] = dk
            total[D:, :] = dv

        @pl.when(jnp.logical_not(self.lows))
        def _():
            dq_ref[pl.ds(self.low, HALF), :] = jnp.zeros((HALF, H * D), BF16)
            dk, dv = self.quadrants((self.high,), keys, dq_ref, False)
            total[:D, :] = dk
            total[D:, :] = dv

    def high_keys(self, keys, dq_ref, total, adds):
        @pl.when(jnp.logical_not(self.lows))
        def _():
            dk, dv = self.quadrants((self.high,), keys, dq_ref, True)
            if adds:
                dk, dv = dk + total[:D, :], dv + total[D:, :]
            total[:D, :] = dk
            total[D:, :] = dv

        if not adds:

            @pl.when(self.lows)
            def _():
                total[...] = jnp.zeros((2 * D, HALF), F32)


def is_even():
    return lax.axis_index("blk") % 2 == 0


def low_kernel(q_ref, g_ref, stat_ref, q2_ref, g2_ref, stat2_ref, own_low, own_high, theirs_low, keep, send, low_total, x_low, x_high, stat_t):
    Queries(q_ref, g_ref, stat_ref, theirs_low, stat_t).low_keys(theirs_low, keep, low_total)
    even = is_even()

    @pl.when(even)
    def _():
        queries = Queries(q2_ref, g2_ref, stat2_ref, own_low, stat_t)
        queries.low_keys(own_low, send, x_low)
        queries.high_keys(own_high, send, x_high, False)

    @pl.when(jnp.logical_not(even))
    def _():
        Queries(q2_ref, g2_ref, stat2_ref, theirs_low, stat_t).low_keys(theirs_low, send, x_low)


def write_back(back, at, total):
    back[at : at + HALF, :] = total[:D, :].T.astype(BF16)
    back[at + HALF : at + T, :] = total[D:, :].T.astype(BF16)


def high_kernel(q_ref, g_ref, stat_ref, q2_ref, g2_ref, stat2_ref, theirs_low, theirs_high, low_total, x_low, _, __, keep, send, back, high_total, stat_t):
    even = is_even()
    Queries(q_ref, g_ref, stat_ref, theirs_low, stat_t).high_keys(
        theirs_high, keep, high_total, False
    )

    @pl.when(even)
    def _():
        write_back(back, 0, low_total[...])

    @pl.when(jnp.logical_not(even))
    def _():
        write_back(back, 0, low_total[...] + x_low[...])
        others = Queries(q2_ref, g2_ref, stat2_ref, theirs_low, stat_t)
        others.high_keys(theirs_high, send, high_total, True)

    write_back(back, T, high_total[...])


def query_kernel(dq_ref, keep_ref, got_ref, out_hbm, out_ref, sems):
    copies = []
    for n in range(4):
        rows = pl.ds(n * T // 4, T // 4)
        total = dq_ref[rows, :] + keep_ref[rows, :].astype(F32) + got_ref[rows, :].astype(F32)
        out_ref[rows, :] = (total * SCALE).astype(BF16)
        copies.append(pltpu.make_async_copy(out_ref.at[rows, :], out_hbm.at[rows, :], sems.at[n]))
        copies[n].start()
    for copy in copies:
        copy.wait()


def key_kernel(own_low, low_total, high_total, got_ref, dk_hbm, dv_hbm, out, sems):
    ql = low_row(piece_of(own_low))
    qh = pl.multiple_of(HALF - ql, HALF)
    copies = []
    for total, rows, at in ((low_total, ql, 0), (high_total, qh, T)):
        for target, n in ((dk_hbm, 0), (dv_hbm, HALF)):
            part = pl.ds(at + n, HALF)
            out[part, :] = (total[n : n + HALF, :] + got_ref[part, :].astype(F32)).astype(BF16)
            to = target.at[pl.ds(rows, HALF), :]
            copies.append(pltpu.make_async_copy(out.at[part, :], to, sems.at[len(copies)]))
            copies[-1].start()
    for copy in copies:
        copy.wait()


def vmem():
    return pl.BlockSpec(memory_space=pltpu.VMEM)


def cost(quadrants, size):
    return pl.CostEstimate(
        flops=int(quadrants * H * 10 * HALF * HALF * D),
        bytes_accessed=size,
        transcendentals=int(quadrants * H * HALF * HALF),
    )


def hbm():
    return pl.BlockSpec(memory_space=pltpu.HBM)


def pack(k, v, positions):
    return pl.pallas_call(
        pack_kernel,
        in_specs=[hbm()] * 3,
        out_specs=vmem(),
        out_shape=jax.ShapeDtypeStruct((2 * T + IDS, D), BF16),
        scratch_shapes=[pltpu.SMEM(positions.shape, jnp.int32), pltpu.SemaphoreType.DMA((3,))],
        name="pack",
    )(k, v, positions)


def hbm():
    return pl.BlockSpec(memory_space=pltpu.HBM)


def in_vmem(value):
    return pltpu.with_memory_space_constraint(value, pltpu.VMEM)


def array(shape, dtype):
    return jax.ShapeDtypeStruct(shape, dtype)


def call(kernel, name, ins, outs, scratch=(), quadrants=0, from_hbm=0, to_hbm=0, aliases=None):
    size = sum(x.size * x.dtype.itemsize for x in list(ins) + list(outs))
    return pl.pallas_call(
        kernel,
        in_specs=[hbm()] * from_hbm + [vmem()] * (len(ins) - from_hbm),
        out_specs=[hbm()] * to_hbm + [vmem()] * (len(outs) - to_hbm),
        out_shape=list(outs),
        scratch_shapes=list(scratch),
        input_output_aliases=aliases or {},
        compiler_params=pltpu.CompilerParams(vmem_limit_bytes=24 << 20),
        cost_estimate=cost(quadrants, size),
        name=name,
    )(*ins)


def passed_along(value, steps):
    count = lax.axis_size("blk")
    pairs = [(source, (source + steps) % count) for source in range(count)]
    return lax.ppermute(value, "blk", pairs)


def swapped(value):
    count = lax.axis_size("blk")
    return lax.ppermute(value, "blk", [(source, source ^ 1) for source in range(count)])


def on_device(q_in, k, v, o, g_in, log_total, positions):
    q_in, k, v, o, g_in, log_total, positions = (
        pltpu.with_memory_space_constraint(x, pltpu.HBM)
        for x in (q_in, k, v, o, g_in, log_total, positions)
    )
    rows = array((T, H * D), BF16)
    stat_t = pltpu.VMEM((T, 3 * H), F32)
    terms, half_terms = array((2 * T, D), F32), array((T, D), F32)
    low, high = call(
        pack_kernel,
        "pack",
        (k, v, positions),
        (array((T + IDS, D), BF16), array((T, D), BF16)),
        (
            pltpu.SMEM(positions.shape, jnp.int32),
            pltpu.VMEM((T, D), BF16),
            pltpu.VMEM((T, D), BF16),
            pltpu.SemaphoreType.DMA((3,)),
        ),
        from_hbm=3,
    )
    theirs_low = in_vmem(passed_along(low, 2))
    low, q_swap, g_swap = lax.optimization_barrier((low, q_in, g_in))
    q2, g2 = in_vmem(swapped(q_swap)), in_vmem(swapped(g_swap))
    q, g, stat = call(
        stat_kernel,
        "stat",
        (q_in, g_in, o, log_total, low),
        (rows, rows, array((3 * H, T), F32)),
        (pltpu.VMEM((T, H * D), BF16), pltpu.VMEM((H, T), F32), pltpu.SemaphoreType.DMA((2, 3))),
        quadrants=30,
        from_hbm=4,
    )
    high, stat = lax.optimization_barrier((high, stat))
    theirs_high = in_vmem(passed_along(high, 2))
    stat2 = in_vmem(swapped(stat))
    own_out = (array((T, H * D), F32), half_terms, half_terms)
    dq, own_low, own_high = call(
        own_ahead_kernel,
        "own_ahead",
        (q, g, stat, low, high),
        own_out,
        (stat_t,),
    )
    theirs_low, dq = lax.optimization_barrier((theirs_low, dq))
    keep, send, low_total, x_low, x_high = call(
        low_kernel,
        "low_keys",
        (q, g, stat, q2, g2, stat2, low, high, theirs_low),
        (rows, rows) + (array((2 * D, HALF), F32),) * 3,
        (stat_t,),
        quadrants=3.5,
    )
    theirs_high, send = lax.optimization_barrier((theirs_high, send))
    keep, send, message_back = call(
        high_kernel,
        "high_keys",
        (q, g, stat, q2, g2, stat2, theirs_low, theirs_high, low_total, x_low, keep, send),
        (rows, rows, array((2 * T, D), BF16)),
        (pltpu.VMEM((2 * D, HALF), F32), stat_t),
        quadrants=0.5,
        aliases={10: 0, 11: 1},
    )
    back = passed_along(message_back, -2)
    got = in_vmem(swapped(send))
    dq, own_low, own_high = call(
        own_kernel,
        "own",
        (q, g, stat, low, high, x_low, x_high, dq, own_low, own_high),
        own_out,
        (stat_t,),
        quadrants=60,
        aliases={7: 0, 8: 1, 9: 2},
    )
    (dq,) = call(
        query_kernel,
        "query_sum",
        (dq, keep, got),
        (rows,),
        (pltpu.VMEM((T, H * D), BF16), pltpu.SemaphoreType.DMA((4,))),
        to_hbm=1,
    )
    back, dq = lax.optimization_barrier((back, dq))
    dk, dv = call(
        key_kernel,
        "key_sum",
        (low, own_low, own_high, back),
        (array((T, D), BF16),) * 2,
        (pltpu.VMEM((2 * T, D), BF16), pltpu.SemaphoreType.DMA((4,))),
        to_hbm=2,
    )
    return dq, dk, dv


def solution(mesh):
    in_specs = (
        P("blk", "tp"),
        P("blk", "tp"),
        P("blk", "tp"),
        P("blk", "tp"),
        P("blk", "tp"),
        P("tp", "blk"),
        P(("blk", "tp")),
    )
    out_specs = (P("blk", "tp"), P("blk", "tp"), P("blk", "tp"))
    return jax.shard_map(
        on_device, mesh=mesh, in_specs=in_specs, out_specs=out_specs, check_vma=False
    )
```
